128 devices in a mesh: row: 8 (over z, x_lo), col: 16 (over y, x_hi, core).
Axes of the slice: x: 4 (x_hi: 2, x_lo: 2; x = x_hi * 2 + x_lo), y: 4, z: 4, core: 2. Of those that a mesh axis runs over, the one named last changes fastest.
Arguments:
- q_halves: float32 [2, 5120, 5120], P(None, 'row', 'col'), may hold values from -6 to 6
- pole_values: float32 [10240], replicated, may hold values from -10240 to 10240, as said below
- weights: float32 [10240], replicated, may hold values from -6 to 6
- secular_roots: float32 [10240], replicated, may hold values from -10240 to 20480, as said below
- column_order: int32 [10240], replicated, may hold values from 0 to 10239, each once
- deflated: int32 [10240], replicated, may hold values 0 or 1
- reflectors: float32 [2, 2, 5120, 256], P(None, None, 'row'), may hold values from -0.0625 to 0.0625
- triangles: float32 [2, 256, 256], replicated, may hold values from -1.5 to 1.5
Outputs:
- eigvecs: float32 [2, 5120, 10240], P(None, 'row', 'col')
The draws below stay inside these ranges and needn't reach their ends.
Inputs may be any that keep to these rules, and one draw needn't show every extreme that they name: `pole_values`: all distinct; sorted, neighbouring poles differ by 0.5 to 1.5. The order of the entries is not sorted. secular_roots[j] lies above pole_values[j], at a quarter to three quarters of the distance to the next larger pole (for the largest pole, of a distance of 0.5 to 1.5), so every pole differs from every root by an eighth or more.
All inputs are finite; a program needn't handle non-finite values.
Results may differ from the reference program's by a relative error of at most 0.00015.
Values sent between devices are 32-bit elements; how exact they have to be, the bound alone decides.
A program may use at most 128 MiB of HBM per device.

```python
import jax
import jax.numpy as jnp
from jax import lax

H = 5120
B = 256
N = 10240


def secular_pair(key):
    base = jax.random.fold_in(key, 4242)
    gaps = jax.random.uniform(jax.random.fold_in(base, 1), (N,), jnp.float32, 0.5, 1.5)
    fracs = jax.random.uniform(jax.random.fold_in(base, 2), (N,), jnp.float32, 0.25, 0.75)
    sorted_poles = jnp.cumsum(gaps) - 0.5 * N
    following = jnp.concatenate([gaps[1:], gaps[:1]])
    sorted_roots = sorted_poles + fracs * following
    shuffle = jax.random.permutation(jax.random.fold_in(base, 3), N)
    return (jnp.take(sorted_poles, shuffle), jnp.take(sorted_roots, shuffle))


def draw_pole_values(key, part):
    return secular_pair(key)[0]


def draw_secular_roots(key, part):
    return secular_pair(key)[1]


def set_ends(drawn, own_key, smallest, largest):
    shape = drawn.shape
    spot = [jax.random.randint(jax.random.fold_in(own_key, axis), (), 0, shape[axis]) for axis in range(len(shape))]
    drawn = drawn.at[tuple(spot)].set(smallest)
    longest = shape.index(max(shape))
    spot[longest] = (spot[longest] + 1) % shape[longest]
    return drawn.at[tuple(spot)].set(largest)


def shard_levels(key, shape, split, low, high):
    factor_of = 1.0
    for position, parts in split:
        draws = jax.random.uniform(jax.random.fold_in(jax.random.fold_in(key, 6), position), (parts,), jnp.float32, low / len(split), high / len(split))
        factor_of = factor_of * jnp.repeat(jnp.exp(draws), shape[position] // parts).reshape((-1,) + (1,) * (len(shape) - 1 - position))
    return factor_of


def bell_draw(rng, extent, width, most, cuts=(), held_as=jnp.bfloat16):
    result = jax.random.normal(rng, extent, jnp.float32) * width
    if len(cuts) > 0:
        result = shard_levels(rng, extent, cuts, -0.22, 0.18) * result
    return jnp.clip(result, min=-most, max=most).astype(held_as)


def setup_inputs(seed: int = 0) -> dict:
    arg_keys = jax.random.split(jax.random.key(seed), 9)
    return {
        "q_halves": bell_draw(arg_keys[0], (2, H, H), 1.0, 6.0, ((1, 8), (2, 16)), jnp.float32),
        "pole_values": draw_pole_values(jax.random.fold_in(arg_keys[8], 71), 0),
        "weights": bell_draw(arg_keys[2], (N,), 1.0, 6.0, (), jnp.float32),
        "secular_roots": draw_secular_roots(jax.random.fold_in(arg_keys[8], 71), 0),
        "column_order": jax.random.permutation(arg_keys[4], N).astype(jnp.int32),
        "deflated": set_ends((jax.random.randint(arg_keys[5], (N,), 0, 4) < 1).astype(jnp.int32), jax.random.fold_in(arg_keys[5], 1), 0, 1),
        "reflectors": bell_draw(arg_keys[6], (2, 2, H, B), N ** -0.5, 0.0625, ((2, 8),), jnp.float32),
        "triangles": bell_draw(arg_keys[7], (2, B, B), 0.25, 1.5, (), jnp.float32),
    }


EPSILON = 1e-06

def column_scale(zeds, pole_values, chosen_roots):
    ratio = zeds[:, None] / (pole_values[:, None] - chosen_roots[None, :])
    return lax.rsqrt(lax.optimization_barrier(jnp.sum(ratio * ratio, axis=0)) + EPSILON)

def cauchy_tile(zeds, pole_values, secular_roots, deflated, first_row, row_count, source, scale):
    pole_slice = lax.dynamic_slice_in_dim(pole_values, first_row, row_count)
    zed_slice = lax.dynamic_slice_in_dim(zeds, first_row, row_count)
    chosen = jnp.take(secular_roots, source)
    cauchy = zed_slice[:, None] / (pole_slice[:, None] - chosen[None, :]) * scale[None, :]
    row_ids = first_row + jnp.arange(row_count, dtype=jnp.int32)
    unit = (row_ids[:, None] == source[None, :]).astype(cauchy.dtype)
    return jnp.where(jnp.take(deflated, source)[None, :] > 0, unit, cauchy)

def project(vectors, field):
    return jnp.einsum('hrb,hrc->bc', vectors, field, precision=lax.Precision.HIGHEST)

def expand(vectors, coef):
    return jnp.einsum('hrb,bc->hrc', vectors, coef, precision=lax.Precision.HIGHEST)

def reference(q_halves, pole_values, weights, secular_roots, column_order, deflated, reflectors, triangles):
    half = q_halves.shape[1]
    zeds = weights * (1 - deflated).astype(weights.dtype)
    scale = column_scale(zeds, pole_values, jnp.take(secular_roots, column_order))
    mixed = jnp.stack([jnp.dot(q_halves[which], cauchy_tile(zeds, pole_values, secular_roots, deflated, which * half, half, column_order, scale), precision=lax.Precision.HIGHEST) for which in range(2)])
    upper = jnp.triu(triangles)
    second = mixed - expand(reflectors[1], jnp.dot(upper[1], project(reflectors[1], mixed), precision=lax.Precision.HIGHEST))
    return second - expand(reflectors[0], jnp.dot(upper[0], project(reflectors[0], second), precision=lax.Precision.HIGHEST))
```

```python
import functools

import jax
import jax.numpy as jnp
from jax import lax
from jax.experimental import pallas as pl
from jax.experimental.pallas import tpu as pltpu
from jax.sharding import PartitionSpec as P

EPSILON = 1e-06
MESH = pl.DeviceIdType.MESH
F32 = jnp.float32
BF16 = jnp.bfloat16
TILE = 320
STRIP = 64


def split(value):
    high = value.astype(BF16)
    return high, (value - high.astype(F32)).astype(BF16)


def dot3(a, b, contract):
    dims = (((contract[0],), (contract[1],)), ((), ()))
    one = functools.partial(lax.dot_general, dimension_numbers=dims, preferred_element_type=F32)
    return one(a[0], b[0]) + one(a[0], b[1]) + one(a[1], b[0])


def merge_kernel(
    q_ref, vec_ref, source_ref, roots_ref, poles_ref, weights_ref, deflated_ref, tri_ref,
    mixed_ref, high_ref, low_ref,
    panel, acc, turned, lam, dfl, squares, c_high, c_low, q_high, q_low,
    proj, proj_in, coef, cross, cross_in, cross_all,
    local_sem, send, recv, row_send, row_recv,
):
    r, col = lax.axis_index("row"), lax.axis_index("col")
    y, x, c = col // 4, lax.rem(col // 2, 2), lax.rem(col, 2)
    width = acc.shape[1]
    piece = width // 8

    def dev(dy, dx, dc):
        return (r, lax.rem(y + dy, 4) * 4 + lax.rem(x + dx, 2) * 2 + lax.rem(c + dc, 2))

    def slot(dy, dx):
        return lax.rem(y + dy, 4) * 2 + lax.rem(x + dx, 2)

    up, down, over, twin = dev(1, 0, 0), dev(3, 0, 0), dev(0, 1, 0), dev(0, 0, 1)
    rows = [(lax.rem(r + d, 8), col) for d in range(1, 8)]

    barrier = pltpu.get_barrier_semaphore()
    for other in [up, down, over, twin, *rows]:
        pl.semaphore_signal(barrier, inc=1, device_id=other, device_id_type=MESH)
    pl.semaphore_wait(barrier, 11)

    started = {}

    def ship(name, src, dst, to):
        at = len(started)
        copy = pltpu.make_async_remote_copy(
            src_ref=src, dst_ref=dst, send_sem=send.at[at], recv_sem=recv.at[at],
            device_id=to, device_id_type=MESH,
        )
        copy.start()
        started[name] = copy

    def relay(name, dy, dx, half, to):
        place = panel.at[slot(dy, dx), half, c]
        ship(name, place, place, to)

    own = []
    for half in range(2):
        place = panel.at[slot(0, 0), half, c]
        ship(("up", half), q_ref.at[half], place, up)
        ship(("down", half), q_ref.at[half], place, down)
        ship(("over", half), q_ref.at[half], place, over)
        ship(("twin", 0, 0, half), q_ref.at[half], place, twin)
        mine = pltpu.make_async_copy(q_ref.at[half], place, local_sem.at[half])
        mine.start()
        own.append(mine)

    total = jnp.zeros(cross.shape, F32)
    for half in range(2):
        total += dot3(split(vec_ref[0, half]), split(vec_ref[1, half]), (0, 0))
    cross[...] = total
    small = cross.shape[0] // 8

    def row_copies(base, src_of, dst):
        copies = []
        for d in range(1, 8):
            to = lax.rem(r + d, 8)
            copy = pltpu.make_async_remote_copy(
                src_ref=src_of(to), dst_ref=dst, send_sem=row_send.at[base + d], recv_sem=row_recv.at[base + d],
                device_id=(to, col), device_id_type=MESH,
            )
            copy.start()
            copies.append(copy)
        return copies

    cross_copies = row_copies(0, lambda to: cross.at[pl.ds(to * small, small)], cross_in.at[r])

    lam[...] = jnp.zeros(lam.shape, F32)
    dfl[...] = jnp.zeros(dfl.shape, F32)
    squares[...] = jnp.zeros(squares.shape, F32)
    span = poles_ref.shape[1]

    def find(step, carry):
        at = step * span + lax.broadcasted_iota(jnp.int32, (1, span), 1)
        root = roots_ref[pl.ds(step, 1), :]
        flag = deflated_ref[pl.ds(step, 1), :].astype(F32)

        def strip(i, inner):
            o = pl.ds(pl.multiple_of(i * STRIP, STRIP), STRIP)
            same = source_ref[o, :] == at
            lam[o, :] += jnp.sum(jnp.where(same, root, 0.0), axis=1, keepdims=True)
            dfl[o, :] += jnp.sum(jnp.where(same, flag, 0.0), axis=1, keepdims=True)
            return inner

        return lax.fori_loop(0, width // STRIP, strip, carry)

    lax.fori_loop(0, 2 * panel.shape[0], find, 0)
    acc[...] = jnp.zeros(acc.shape, F32)

    def unit(m, half):
        line = half * 8 + m
        pole = poles_ref[pl.ds(line, 1), :]
        zed = weights_ref[pl.ds(line, 1), :] * (1 - deflated_ref[pl.ds(line, 1), :]).astype(F32)
        at = line * span + lax.broadcasted_iota(jnp.int32, (1, span), 1)
        q_high[...], q_low[...] = split(panel[m, half].reshape(span, width))

        def tile(t, carry):
            def strip(i, inner):
                o = pl.ds(pl.multiple_of(t * TILE + i * STRIP, STRIP), STRIP)
                value = zed / (pole - lam[o, :])
                squares[o, :] += jnp.sum(value * value, axis=1, keepdims=True)
                single = jnp.where(source_ref[o, :] == at, 1.0, 0.0)
                value = jnp.where(dfl[o, :] > 0, single, value)
                into = pl.ds(pl.multiple_of(i * STRIP, STRIP), STRIP)
                c_high[into, :], c_low[into, :] = split(value)
                return inner

            lax.fori_loop(0, TILE // STRIP, strip, 0)
            o = pl.ds(pl.multiple_of(t * TILE, TILE), TILE)
            acc[half, o, :] += dot3((c_high[...], c_low[...]), (q_high[...], q_low[...]), (1, 0))
            return carry

        lax.fori_loop(0, width // TILE, tile, 0)

    def both(step, carry):
        unit(slot(0, 0), step)
        return carry

    for half in range(2):
        own[half].wait()
        started["twin", 0, 0, half].wait_recv()
    lax.fori_loop(0, 2, both, 0)

    for copy in cross_copies:
        copy.wait()
    mine = pl.ds(r * small, small)
    total = cross[mine, :]
    for d in range(1, 8):
        total += cross_in[lax.rem(r + d, 8)]
    cross_all[mine, :] = total
    cross_copies = row_copies(8, lambda to: cross_all.at[mine], cross_all.at[mine])

    def arrive(name, dy, dx, half):
        started[name].wait_recv()
        relay(("twin", dy, dx, half), dy, dx, half, twin)

    def three(half):
        for dy, dx in ((3, 0), (1, 0), (0, 1)):
            started["twin", dy, dx, half].wait_recv()

        def one(i, carry):
            dx = i // 2
            unit(slot(3 - 2 * i + dx, dx), half)
            return carry

        lax.fori_loop(0, 3, one, 0)

    arrive(("up", 0), 3, 0, 0)
    relay(("up2", 0), 3, 0, 0, up)
    arrive(("over", 0), 0, 1, 0)
    relay(("upx", 0), 0, 1, 0, up)
    relay(("downx", 0), 0, 1, 0, down)
    arrive(("down", 0), 1, 0, 0)
    arrive(("down", 1), 1, 0, 1)
    relay(("down2", 1), 1, 0, 1, down)
    arrive(("over", 1), 0, 1, 1)
    relay(("upx", 1), 0, 1, 1, up)
    relay(("downx", 1), 0, 1, 1, down)
    arrive(("up", 1), 3, 0, 1)
    three(0)
    arrive(("up2", 0), 2, 0, 0)
    relay(("over2", 0), 2, 0, 0, over)
    three(1)
    arrive(("down2", 1), 2, 0, 1)
    relay(("over2", 1), 2, 0, 1, over)

    def pair(dys, dx, halves):
        for dy in dys:
            for half in halves:
                started["twin", dy, dx, half].wait_recv()

        def one(i, carry):
            dy = dys[0] + i * (dys[-1] - dys[0])
            unit(slot(dy, dx), halves[0] + i * (halves[-1] - halves[0]))
            return carry

        lax.fori_loop(0, len(dys) * len(halves), one, 0)

    pair((2,), 0, (0, 1))
    for half in range(2):
        arrive(("upx", half), 3, 1, half)
        arrive(("downx", half), 1, 1, half)
        pair((1, 3), 1, (half,))
    arrive(("over2", 0), 2, 1, 0)
    arrive(("over2", 1), 2, 1, 1)
    pair((2,), 1, (0, 1))

    size = vec_ref.shape[3]
    factor = jnp.where(dfl[...] > 0, 1.0, lax.rsqrt(squares[...] + EPSILON))
    lam[...] = factor

    def project(t, carry):
        o = pl.ds(pl.multiple_of(t * TILE, TILE), TILE)
        got = []
        for half in range(2):
            value = acc[half, o, :] * lam[o, :]
            acc[half, o, :] = value
            got.append(split(value))
        for block in range(2):
            proj[o, block * size : (block + 1) * size] = dot3(
                got[0], split(vec_ref[block, 0]), (1, 0)
            ) + dot3(got[1], split(vec_ref[block, 1]), (1, 0))
        return carry

    lax.fori_loop(0, width // TILE, project, 0)
    proj_copies = row_copies(16, lambda to: proj.at[pl.ds(to * piece, piece)], proj_in.at[r])

    for half in range(2):
        turned[half] = acc[half].T
    out = pltpu.make_async_copy(turned, mixed_ref, local_sem.at[2])
    out.start()

    for copy in cross_copies:
        copy.wait()
    for copy in proj_copies:
        copy.wait()
    mine = pl.ds(r * piece, piece)
    total = proj[mine, :]
    for d in range(1, 8):
        total += proj_in[lax.rem(r + d, 8)]
    order = [lax.broadcasted_iota(jnp.int32, (size, size), i) for i in range(2)]
    upper = [split(jnp.where(order[0] <= order[1], tri_ref[i], 0.0)) for i in range(2)]
    second = dot3(split(total[:, size:]), upper[1], (1, 1))
    rest = total[:, :size] - dot3(split(second), split(cross_all[...]), (1, 1))
    coef[mine, :size] = dot3(split(rest), upper[0], (1, 1))
    coef[mine, size:] = second
    for copy in row_copies(24, lambda to: coef.at[mine], coef.at[mine]):
        copy.wait()
    high_ref[...], low_ref[...] = split(coef[...])
    for copy in started.values():
        copy.wait_send()
    out.wait()


def merge(q_turned, vectors, source, roots, poles, weights, deflated, triangles):
    depth, width = q_turned.shape[1], q_turned.shape[2]
    size = vectors.shape[3]
    vmem = pl.BlockSpec(memory_space=pltpu.VMEM)
    hbm = pl.BlockSpec(memory_space=pl.ANY)
    dma = pltpu.SemaphoreType.DMA
    span = 2 * depth
    return pl.pallas_call(
        merge_kernel,
        out_shape=(
            jax.ShapeDtypeStruct((2, width, width), F32),
            jax.ShapeDtypeStruct((width, 2 * size), BF16),
            jax.ShapeDtypeStruct((width, 2 * size), BF16),
        ),
        in_specs=[hbm] + [vmem] * 7,
        out_specs=(hbm, vmem, vmem),
        scratch_shapes=[
            pltpu.VMEM((8, 2, 2, depth, width), F32),
            pltpu.VMEM((2, width, width), F32),
            pltpu.VMEM((2, width, width), F32),
            pltpu.VMEM((width, 1), F32),
            pltpu.VMEM((width, 1), F32),
            pltpu.VMEM((width, 1), F32),
            pltpu.VMEM((TILE, span), BF16),
            pltpu.VMEM((TILE, span), BF16),
            pltpu.VMEM((span, width), BF16),
            pltpu.VMEM((span, width), BF16),
            pltpu.VMEM((width, 2 * size), F32),
            pltpu.VMEM((8, width // 8, 2 * size), F32),
            pltpu.VMEM((width, 2 * size), F32),
            pltpu.VMEM((size, size), F32),
            pltpu.VMEM((8, size // 8, size), F32),
            pltpu.VMEM((size, size), F32),
            dma((3,)),
            dma((32,)),
            dma((32,)),
            dma((32,)),
            dma((32,)),
        ],
        compiler_params=pltpu.CompilerParams(
            collective_id=0, has_side_effects=True, vmem_limit_bytes=60 * 1024 * 1024
        ),
        name="merge",
    )(q_turned, vectors, source, roots, poles, weights, deflated, triangles)


def update_kernel(mixed_ref, vec_ref, high_ref, low_ref, out_ref):
    size = vec_ref.shape[3]
    total = mixed_ref[0]
    for block in range(2):
        take = slice(block * size, (block + 1) * size)
        total -= dot3(split(vec_ref[block, 0]), (high_ref[:, take], low_ref[:, take]), (1, 1))
    out_ref[0] = total


def update(mixed, vectors, high, low):
    _, height, width = mixed.shape
    size = vectors.shape[3]
    part = 320
    whole = pl.BlockSpec((width, 2 * size), lambda h, i: (0, 0))
    return pl.pallas_call(
        update_kernel,
        grid=(2, height // part),
        out_shape=jax.ShapeDtypeStruct(mixed.shape, F32),
        in_specs=[
            pl.BlockSpec((1, part, width), lambda h, i: (h, i, 0)),
            pl.BlockSpec((2, 1, part, size), lambda h, i: (0, h, i, 0)),
            whole,
            whole,
        ],
        out_specs=pl.BlockSpec((1, part, width), lambda h, i: (h, i, 0)),
        compiler_params=pltpu.CompilerParams(vmem_limit_bytes=32 * 1024 * 1024),
        name="update",
    )(mixed, vectors, high, low)


def local(
    q_halves, pole_values, weights, secular_roots, column_order, deflated, reflectors, triangles
):
    depth = q_halves.shape[2]
    col = lax.axis_index("col")
    source = lax.dynamic_slice_in_dim(column_order, col * 2 * depth, 2 * depth).reshape(-1, 1)
    lines = (16, 2 * depth)
    mixed, high, low = merge(
        jnp.swapaxes(q_halves, 1, 2),
        reflectors,
        source,
        secular_roots.reshape(lines),
        pole_values.reshape(lines),
        weights.reshape(lines),
        deflated.reshape(lines),
        triangles,
    )
    return update(mixed, reflectors, high, low)


def solution(mesh):
    placed = (P(None, "row", "col"), P(), P(), P(), P(), P(), P(None, None, "row", None), P())
    return jax.shard_map(
        local, mesh=mesh, in_specs=placed, out_specs=P(None, "row", "col"), check_vma=False
    )
```

```python
import functools

import jax
import jax.numpy as jnp
from jax import lax
from jax.experimental import pallas as pl
from jax.experimental.pallas import tpu as pltpu
from jax.sharding import PartitionSpec as P

EPSILON = 1e-06
MESH = pl.DeviceIdType.MESH
F32 = jnp.float32
BF16 = jnp.bfloat16
TILE = 320
LANES = 128
STRIP = 64


def split(value):
    high = value.astype(BF16)
    return high, (value - high.astype(F32)).astype(BF16)


def dot3(a, b, contract):
    dims = (((contract[0],), (contract[1],)), ((), ()))
    one = functools.partial(lax.dot_general, dimension_numbers=dims, preferred_element_type=F32)
    return one(a[0], b[0]) + one(a[0], b[1]) + one(a[1], b[0])


def merge_kernel(
    q_ref, vec_ref, order_ref, roots_ref, lines_ref, weights_ref, deflated_ref, tri_ref,
    mixed_ref, high_ref, low_ref,
    panel, acc, turned, poles_ref, zeds_ref, source, lam, keep, squares, c_high, c_low, q_high, q_low,
    proj, proj_in, coef, cross, cross_in, cross_all,
    local_sem, send, recv, row_send, row_recv,
):
    r, col = lax.axis_index("row"), lax.axis_index("col")
    y, x, c = col // 4, lax.rem(col // 2, 2), lax.rem(col, 2)
    width = acc.shape[1]
    piece = width // 8

    def dev(dy, dx, dc):
        return (r, lax.rem(y + dy, 4) * 4 + lax.rem(x + dx, 2) * 2 + lax.rem(c + dc, 2))

    def slot(dy, dx):
        return lax.rem(y + dy, 4) * 2 + lax.rem(x + dx, 2)

    up, down, over, twin = dev(1, 0, 0), dev(3, 0, 0), dev(0, 1, 0), dev(0, 0, 1)
    rows = [(lax.rem(r + d, 8), col) for d in range(1, 8)]

    barrier = pltpu.get_barrier_semaphore()
    for other in [up, down, over, twin, *rows]:
        pl.semaphore_signal(barrier, inc=1, device_id=other, device_id_type=MESH)
    pl.semaphore_wait(barrier, 11)

    started = {}

    def ship(name, src, dst, to):
        at = len(started)
        copy = pltpu.make_async_remote_copy(
            src_ref=src, dst_ref=dst, send_sem=send.at[at], recv_sem=recv.at[at],
            device_id=to, device_id_type=MESH,
        )
        copy.start()
        started[name] = copy

    def relay(name, dy, dx, half, to):
        place = panel.at[slot(dy, dx), half, c]
        ship(name, place, place, to)

    own = []
    for half in range(2):
        place = panel.at[slot(0, 0), half, c]
        mine = pltpu.make_async_copy(q_ref.at[half], place, local_sem.at[half])
        mine.start()
        own.append(mine)
        ship(("up", half), q_ref.at[half], place, up)
        other = panel.at[slot(0, 0), 1 - half, c]
        ship(("down", 1 - half), q_ref.at[1 - half], other, down)
        ship(("twin", 0, 0, half), q_ref.at[half], place, twin)

    total = jnp.zeros(cross.shape, F32)
    for half in range(2):
        total += dot3(split(vec_ref[0, half]), split(vec_ref[1, half]), (0, 0))
    cross[...] = total
    small = cross.shape[0] // 8

    def row_copies(base, src_of, dst):
        copies = []
        for d in range(1, 8):
            to = lax.rem(r + d, 8)
            copy = pltpu.make_async_remote_copy(
                src_ref=src_of(to), dst_ref=dst, send_sem=row_send.at[base + d], recv_sem=row_recv.at[base + d],
                device_id=(to, col), device_id_type=MESH,
            )
            copy.start()
            copies.append(copy)
        return copies

    cross_copies = row_copies(0, lambda to: cross.at[pl.ds(to * small, small)], cross_in.at[r])

    for half in range(2):
        ship(("over", half), q_ref.at[half], panel.at[slot(0, 0), half, c], over)

    span = 2 * panel.shape[3]
    group = span // LANES
    for line in range(2 * panel.shape[0]):
        for i in range(group):
            at = slice(line * group + i, line * group + i + 1)
            into = (slice(line, line + 1), slice(i * LANES, (i + 1) * LANES))
            poles_ref[into] = lines_ref[at, :]
            zeds_ref[into] = weights_ref[at, :] * (1 - deflated_ref[at, :]).astype(F32)

    squares[...] = jnp.zeros(squares.shape, F32)
    acc[...] = jnp.zeros(acc.shape, F32)
    for i in range(width // LANES):
        own_line = order_ref[pl.ds(col * (width // LANES) + i, 1), :].astype(F32)
        source[i * LANES : (i + 1) * LANES, :] = jnp.broadcast_to(own_line, (LANES, LANES)).T

    def find(i, carry):
        o = pl.ds(pl.multiple_of(i * STRIP, STRIP), STRIP)
        wanted = source[o, :].astype(jnp.int32)

        def line(step, found):
            same = wanted == step * LANES + lax.broadcasted_iota(jnp.int32, (1, LANES), 1)
            flag = deflated_ref[pl.ds(step, 1), :].astype(F32)
            return (
                found[0] + jnp.where(same, roots_ref[pl.ds(step, 1), :], 0.0),
                found[1] + jnp.where(same, flag, 0.0),
            )

        zero = jnp.zeros((STRIP, LANES), F32)
        root, flag = lax.fori_loop(0, roots_ref.shape[0], line, (zero, zero))
        flag = jnp.sum(flag, axis=1, keepdims=True)
        lam[o, :] = jnp.broadcast_to(jnp.sum(root, axis=1, keepdims=True), (STRIP, LANES))
        keep[o, :] = jnp.broadcast_to(1.0 - flag, (STRIP, LANES))
        source[o, :] = jnp.where(flag > 0, source[o, :], -1.0)
        return carry

    lax.fori_loop(0, width // STRIP, find, 0)

    def unit(m, half):
        at = half * 8 + m
        pole = poles_ref[pl.ds(at, 1), :]
        zed = zeds_ref[pl.ds(at, 1), :]
        count = (at * span + lax.broadcasted_iota(jnp.int32, (1, span), 1)).astype(F32)
        q_high[...], q_low[...] = split(panel[m, half].reshape(span, width))
        for t in range(width // TILE):
            for i in range(TILE // STRIP):
                o = slice(t * TILE + i * STRIP, t * TILE + (i + 1) * STRIP)
                into = slice(i * STRIP, (i + 1) * STRIP)
                total = squares[o, :]
                for k in range(group):
                    lanes = slice(k * LANES, (k + 1) * LANES)
                    gap = pole[:, lanes] - lam[o, :]
                    guess = pl.reciprocal(gap, approx=True)
                    guess = guess * (2.0 - gap * guess)
                    value = zed[:, lanes] * guess
                    total += value * value
                    value = jnp.where(source[o, :] == count[:, lanes], 1.0, value * keep[o, :])
                    c_high[t, into, lanes], c_low[t, into, lanes] = split(value)
                squares[o, :] = total
        for t in range(width // TILE):
            o = slice(t * TILE, (t + 1) * TILE)
            acc[half, o, :] += dot3((c_high[t], c_low[t]), (q_high[...], q_low[...]), (1, 0))

    def run(steps, place):
        def one(i, carry):
            dy, dx, half = place(i)
            unit(slot(dy, dx), half)
            return carry

        lax.fori_loop(0, steps, one, 0)

    def arrive(name, dy, dx, half):
        started[name].wait_recv()
        relay(("twin", dy, dx, half), dy, dx, half, twin)

    def ready(*places):
        for dy, dx, half in places:
            started["twin", dy, dx, half].wait_recv()

    for half in range(2):
        own[half].wait()
    ready((0, 0, 0), (0, 0, 1))
    run(2, lambda i: (0, 0, i))

    arrive(("up", 0), 3, 0, 0)
    relay(("up2", 0), 3, 0, 0, up)
    arrive(("down", 1), 1, 0, 1)
    relay(("down2", 1), 1, 0, 1, down)
    arrive(("over", 0), 0, 1, 0)
    relay(("upx", 0), 0, 1, 0, up)
    relay(("downx", 0), 0, 1, 0, down)
    ready((3, 0, 0), (1, 0, 1), (0, 1, 0))
    run(3, lambda i: (3 - 2 * i + i // 2, i // 2, lax.rem(i, 2)))

    for copy in cross_copies:
        copy.wait()
    mine = pl.ds(r * small, small)
    total = cross[mine, :]
    for d in range(1, 8):
        total += cross_in[lax.rem(r + d, 8)]
    cross_all[mine, :] = total
    cross_copies = row_copies(8, lambda to: cross_all.at[mine], cross_all.at[mine])

    arrive(("up", 1), 3, 0, 1)
    arrive(("down", 0), 1, 0, 0)
    arrive(("over", 1), 0, 1, 1)
    relay(("upx", 1), 0, 1, 1, up)
    relay(("downx", 1), 0, 1, 1, down)
    ready((3, 0, 1), (1, 0, 0), (0, 1, 1))
    run(3, lambda i: (3 - 2 * i + i // 2, i // 2, 1 - lax.rem(i, 2)))

    arrive(("up2", 0), 2, 0, 0)
    relay(("over2", 0), 2, 0, 0, over)
    arrive(("down2", 1), 2, 0, 1)
    relay(("over2", 1), 2, 0, 1, over)
    ready((2, 0, 0), (2, 0, 1))
    run(2, lambda i: (2, 0, i))

    for half in range(2):
        arrive(("upx", half), 3, 1, half)
        arrive(("downx", half), 1, 1, half)
        arrive(("over2", half), 2, 1, half)
        ready((3, 1, half), (1, 1, half), (2, 1, half))
        run(3, lambda i, half=half: (3 - 2 * i + 3 * (i // 2), 1, half))

    size = vec_ref.shape[3]
    norm = lax.rsqrt(jnp.sum(squares[...], axis=1, keepdims=True) + EPSILON)
    lam[...] = jnp.where(keep[...] > 0, norm, 1.0)

    def project(t, carry):
        o = pl.ds(pl.multiple_of(t * TILE, TILE), TILE)
        got = []
        for half in range(2):
            value = acc[half, o, :] * lam[o, :1]
            acc[half, o, :] = value
            got.append(split(value))
        for block in range(2):
            proj[o, block * size : (block + 1) * size] = dot3(
                got[0], split(vec_ref[block, 0]), (1, 0)
            ) + dot3(got[1], split(vec_ref[block, 1]), (1, 0))
        return carry

    lax.fori_loop(0, width // TILE, project, 0)
    proj_copies = row_copies(16, lambda to: proj.at[pl.ds(to * piece, piece)], proj_in.at[r])

    for half in range(2):
        turned[half] = acc[half].T
    out = pltpu.make_async_copy(turned, mixed_ref, local_sem.at[2])
    out.start()

    for copy in cross_copies:
        copy.wait()
    for copy in proj_copies:
        copy.wait()
    mine = pl.ds(r * piece, piece)
    total = proj[mine, :]
    for d in range(1, 8):
        total += proj_in[lax.rem(r + d, 8)]
    order = [lax.broadcasted_iota(jnp.int32, (size, size), i) for i in range(2)]
    upper = [split(jnp.where(order[0] <= order[1], tri_ref[i], 0.0)) for i in range(2)]
    second = dot3(split(total[:, size:]), upper[1], (1, 1))
    rest = total[:, :size] - dot3(split(second), split(cross_all[...]), (1, 1))
    coef[mine, :size] = dot3(split(rest), upper[0], (1, 1))
    coef[mine, size:] = second
    for copy in row_copies(24, lambda to: coef.at[mine], coef.at[mine]):
        copy.wait()
    high_ref[...], low_ref[...] = split(coef[...])
    for copy in started.values():
        copy.wait_send()
    out.wait()


def merge(q_turned, vectors, order, roots, poles, weights, deflated, triangles):
    depth, width = q_turned.shape[1], q_turned.shape[2]
    size = vectors.shape[3]
    vmem = pl.BlockSpec(memory_space=pltpu.VMEM)
    hbm = pl.BlockSpec(memory_space=pl.ANY)
    dma = pltpu.SemaphoreType.DMA
    span = 2 * depth
    return pl.pallas_call(
        merge_kernel,
        out_shape=(
            jax.ShapeDtypeStruct((2, width, width), F32),
            jax.ShapeDtypeStruct((width, 2 * size), BF16),
            jax.ShapeDtypeStruct((width, 2 * size), BF16),
        ),
        in_specs=[hbm] + [vmem] * 7,
        out_specs=(hbm, vmem, vmem),
        scratch_shapes=[
            pltpu.VMEM((8, 2, 2, depth, width), F32),
            pltpu.VMEM((2, width, width), F32),
            pltpu.VMEM((2, width, width), F32),
            pltpu.VMEM((16, span), F32),
            pltpu.VMEM((16, span), F32),
            pltpu.VMEM((width, LANES), F32),
            pltpu.VMEM((width, LANES), F32),
            pltpu.VMEM((width, LANES), F32),
            pltpu.VMEM((width, LANES), F32),
            pltpu.VMEM((width // TILE, TILE, span), BF16),
            pltpu.VMEM((width // TILE, TILE, span), BF16),
            pltpu.VMEM((span, width), BF16),
            pltpu.VMEM((span, width), BF16),
            pltpu.VMEM((width, 2 * size), F32),
            pltpu.VMEM((8, width // 8, 2 * size), F32),
            pltpu.VMEM((width, 2 * size), F32),
            pltpu.VMEM((size, size), F32),
            pltpu.VMEM((8, size // 8, size), F32),
            pltpu.VMEM((size, size), F32),
            dma((3,)),
            dma((32,)),
            dma((32,)),
            dma((32,)),
            dma((32,)),
        ],
        compiler_params=pltpu.CompilerParams(
            collective_id=0, has_side_effects=True, vmem_limit_bytes=60 * 1024 * 1024
        ),
        name="merge",
    )(q_turned, vectors, order, roots, poles, weights, deflated, triangles)


def update_kernel(mixed_ref, vec_ref, high_ref, low_ref, out_ref):
    size = vec_ref.shape[3]
    total = mixed_ref[0]
    for block in range(2):
        take = slice(block * size, (block + 1) * size)
        total -= dot3(split(vec_ref[block, 0]), (high_ref[:, take], low_ref[:, take]), (1, 1))
    out_ref[0] = total


def update(mixed, vectors, high, low):
    _, height, width = mixed.shape
    size = vectors.shape[3]
    part = 320
    whole = pl.BlockSpec((width, 2 * size), lambda h, i: (0, 0))
    return pl.pallas_call(
        update_kernel,
        grid=(2, height // part),
        out_shape=jax.ShapeDtypeStruct(mixed.shape, F32),
        in_specs=[
            pl.BlockSpec((1, part, width), lambda h, i: (h, i, 0)),
            pl.BlockSpec((2, 1, part, size), lambda h, i: (0, h, i, 0)),
            whole,
            whole,
        ],
        out_specs=pl.BlockSpec((1, part, width), lambda h, i: (h, i, 0)),
        compiler_params=pltpu.CompilerParams(vmem_limit_bytes=32 * 1024 * 1024),
        name="update",
    )(mixed, vectors, high, low)


def local(
    q_halves, pole_values, weights, secular_roots, column_order, deflated, reflectors, triangles
):
    lines = (-1, LANES)
    mixed, high, low = merge(
        jnp.swapaxes(q_halves, 1, 2),
        reflectors,
        column_order.reshape(lines),
        secular_roots.reshape(lines),
        pole_values.reshape(lines),
        weights.reshape(lines),
        deflated.reshape(lines),
        triangles,
    )
    return update(mixed, reflectors, high, low)


def solution(mesh):
    placed = (P(None, "row", "col"), P(), P(), P(), P(), P(), P(None, None, "row", None), P())
    return jax.shard_map(
        local, mesh=mesh, in_specs=placed, out_specs=P(None, "row", "col"), check_vma=False
    )
```

```python
import functools

import jax
import jax.numpy as jnp
from jax import lax
from jax.experimental import pallas as pl
from jax.experimental.pallas import tpu as pltpu
from jax.sharding import PartitionSpec as P

EPSILON = 1e-06
MESH = pl.DeviceIdType.MESH
F32 = jnp.float32
BF16 = jnp.bfloat16
TILE = 320
LANES = 128
STRIP = 64


def split(value):
    high = value.astype(BF16)
    return high, (value - high.astype(F32)).astype(BF16)


def dot3(a, b, contract):
    dims = (((contract[0],), (contract[1],)), ((), ()))
    one = functools.partial(lax.dot_general, dimension_numbers=dims, preferred_element_type=F32)
    return one(a[0], b[0]) + one(a[0], b[1]) + one(a[1], b[0])


def merge_kernel(
    q_ref, vec_ref, order_ref, roots_ref, lines_ref, weights_ref, deflated_ref, tri_ref,
    turned_ref,
    panel, acc, poles_ref, zeds_ref, pole_cols, zed_cols, marks, source, lam, keep, squares,
    c_high, c_low, q_high, q_low, wall, proj, z_in, part, x_in, coef, cross, cross_in, cross_all,
    local_sem, send, recv, row_send, row_recv,
):
    r, col = lax.axis_index("row"), lax.axis_index("col")
    y, x, c = col // 4, lax.rem(col // 2, 2), lax.rem(col, 2)
    width = acc.shape[1]
    piece = width // 8
    z, low = r // 2, lax.rem(r, 2)
    size = vec_ref.shape[3]

    def dev(dy, dx, dc):
        return (r, lax.rem(y + dy, 4) * 4 + lax.rem(x + dx, 2) * 2 + lax.rem(c + dc, 2))

    def slot(dy, dx):
        return lax.rem(y + dy, 4) * 2 + lax.rem(x + dx, 2)

    up, down, over, twin = dev(1, 0, 0), dev(3, 0, 0), dev(0, 1, 0), dev(0, 0, 1)
    rows = [(lax.rem(r + d, 8), col) for d in range(1, 8)]

    barrier = pltpu.get_barrier_semaphore()
    for other in [up, down, dev(2, 0, 0), over, twin, *rows]:
        pl.semaphore_signal(barrier, inc=1, device_id=other, device_id_type=MESH)
    pl.semaphore_wait(barrier, 12)

    started = {}

    def ship(name, src, dst, to):
        at = len(started)
        copy = pltpu.make_async_remote_copy(
            src_ref=src, dst_ref=dst, send_sem=send.at[at], recv_sem=recv.at[at],
            device_id=to, device_id_type=MESH,
        )
        copy.start()
        started[name] = copy
        return copy

    def relay(name, dy, dx, half, to):
        place = panel.at[slot(dy, dx), half, c]
        ship(name, place, place, to)

    own = []
    for half in range(2):
        place = panel.at[slot(0, 0), half, c]
        mine = pltpu.make_async_copy(q_ref.at[half], place, local_sem.at[half])
        mine.start()
        own.append(mine)
        ship(("up", half), q_ref.at[half], place, up)
        other = panel.at[slot(0, 0), 1 - half, c]
        ship(("down", 1 - half), q_ref.at[1 - half], other, down)
        ship(("twin", 0, 0, half), q_ref.at[half], place, twin)
    ship(("over", 0), q_ref.at[0], panel.at[slot(0, 0), 0, c], over)

    total = jnp.zeros(cross.shape, F32)
    for half in range(2):
        total += dot3(split(vec_ref[0, half]), split(vec_ref[1, half]), (0, 0))
    cross[...] = total
    small = cross.shape[0] // 8

    def row_copies(base, src_of, dst):
        copies = []
        for d in range(1, 8):
            to = lax.rem(r + d, 8)
            copy = pltpu.make_async_remote_copy(
                src_ref=src_of(to), dst_ref=dst, send_sem=row_send.at[base + d], recv_sem=row_recv.at[base + d],
                device_id=(to, col), device_id_type=MESH,
            )
            copy.start()
            copies.append(copy)
        return copies

    cross_copies = row_copies(0, lambda to: cross.at[pl.ds(to * small, small)], cross_in.at[r])

    def one_row(at, src, dst, to):
        copy = pltpu.make_async_remote_copy(
            src_ref=src, dst_ref=dst, send_sem=row_send.at[at], recv_sem=row_recv.at[at],
            device_id=(to, col), device_id_type=MESH,
        )
        copy.start()
        return copy

    def scatter_z(base, which):
        copies = []
        for d in range(1, 4):
            to = lax.rem(z + d, 4)
            src = proj.at[which, pl.ds(to * 2 * piece, 2 * piece)]
            copies.append(one_row(base + d, src, z_in.at[which, z], to * 2 + low))
        return copies

    def scatter_x(base, which, copies):
        for copy in copies:
            copy.wait()
        total = proj[which, pl.ds(z * 2 * piece, 2 * piece), :]
        for d in range(1, 4):
            total += z_in[which, lax.rem(z + d, 4)]
        part[which] = total
        src = part.at[which, pl.ds((1 - low) * piece, piece)]
        return one_row(base, src, x_in.at[which], z * 2 + 1 - low)

    depth = panel.shape[3]
    for half in range(2):
        own[half].wait()
        got = split(panel[slot(0, 0), half, c])
        for block in range(2):
            at = (0, slice(half * depth, (half + 1) * depth), slice(block * size, (block + 1) * size))
            proj[at] = dot3(got, split(vec_ref[block, half]), (1, 0))
    w_copies = scatter_z(16, 0)

    span = 2 * panel.shape[3]
    group = span // LANES
    for line in range(2 * panel.shape[0]):
        for i in range(group):
            at = slice(line * group + i, line * group + i + 1)
            into = (slice(line, line + 1), slice(i * LANES, (i + 1) * LANES))
            poles_ref[into] = lines_ref[at, :]
            zeds_ref[into] = weights_ref[at, :] * (1 - deflated_ref[at, :]).astype(F32)

    squares[...] = jnp.zeros(squares.shape, F32)
    acc[...] = jnp.zeros(acc.shape, F32)
    for i in range(width // LANES):
        own_line = order_ref[pl.ds(col * (width // LANES) + i, 1), :].astype(F32)
        source[i * LANES : (i + 1) * LANES, :] = jnp.broadcast_to(own_line, (LANES, LANES)).T

    def find(i, carry):
        o = pl.ds(pl.multiple_of(i * STRIP, STRIP), STRIP)
        wanted = source[o, :].astype(jnp.int32)

        def line(step, found):
            same = wanted == step * LANES + lax.broadcasted_iota(jnp.int32, (1, LANES), 1)
            flag = deflated_ref[pl.ds(step, 1), :].astype(F32)
            return (
                found[0] + jnp.where(same, roots_ref[pl.ds(step, 1), :], 0.0),
                found[1] + jnp.where(same, flag, 0.0),
            )

        zero = jnp.zeros((STRIP, LANES), F32)
        root, flag = lax.fori_loop(0, roots_ref.shape[0], line, (zero, zero))
        flag = jnp.sum(flag, axis=1, keepdims=True)
        lam[o, :] = jnp.broadcast_to(jnp.sum(root, axis=1, keepdims=True), (STRIP, LANES))
        keep[o, :] = jnp.broadcast_to(1.0 - flag, (STRIP, LANES))
        source[o, :] = jnp.where(flag > 0, source[o, :], -1.0)
        return carry

    lax.fori_loop(0, width // STRIP, find, 0)

    w_copy = scatter_x(20, 0, w_copies)
    ship(("over", 1), q_ref.at[1], panel.at[slot(0, 0), 1, c], over)
    for i in range(width // LANES):
        o = slice(i * LANES, (i + 1) * LANES)
        for line, values in enumerate((lam, keep, source)):
            marks[line : line + 1, o] = values[o, :].T[:1, :]
    for i in range(group):
        o = slice(i * LANES, (i + 1) * LANES)
        for half in range(2):
            pole_cols[half, o, :] = poles_ref[half * 8 : (half + 1) * 8, o].T
            zed_cols[half, o, :] = zeds_ref[half * 8 : (half + 1) * 8, o].T

    def coefficients(core, carry):
        half, first = r // 4, core * depth + lax.rem(r, 4) * piece
        lines = pl.ds(pl.multiple_of(first, 16), piece)
        inner = lax.broadcasted_iota(jnp.int32, (piece, 1), 0)
        for dx in range(2):
            for dy in range(4):
                m = dy * 2 + dx
                pole = pole_cols[half, lines, m : m + 1]
                zed = zed_cols[half, lines, m : m + 1]
                count = (half * 8 * span + m * span + first + inner).astype(F32)
                into = slice((dx * 4 + dy) * piece, (dx * 4 + dy + 1) * piece)
                for i in range(width // LANES):
                    o = slice(i * LANES, (i + 1) * LANES)
                    gap = pole - marks[0:1, o]
                    guess = pl.reciprocal(gap, approx=True)
                    guess = guess * (2.0 - gap * guess)
                    value = zed * guess * marks[1:2, o]
                    value = jnp.where(marks[2:3, o] == count, 1.0, value)
                    q_high[into, o], q_low[into, o] = split(value)
        w = split(wall[core].reshape(8 * piece, 2 * size))
        proj[1] += dot3((q_high[...], q_low[...]), w, (0, 0))
        return carry

    def unit(m, half):
        at = half * 8 + m
        pole = poles_ref[pl.ds(at, 1), :]
        zed = zeds_ref[pl.ds(at, 1), :]
        count = (at * span + lax.broadcasted_iota(jnp.int32, (1, span), 1)).astype(F32)
        q_high[...], q_low[...] = split(panel[m, half].reshape(span, width))
        for t in range(width // TILE):
            for i in range(TILE // STRIP):
                o = slice(t * TILE + i * STRIP, t * TILE + (i + 1) * STRIP)
                into = slice(i * STRIP, (i + 1) * STRIP)
                total = squares[o, :]
                for k in range(group):
                    lanes = slice(k * LANES, (k + 1) * LANES)
                    gap = pole[:, lanes] - lam[o, :]
                    guess = pl.reciprocal(gap, approx=True)
                    guess = guess * (2.0 - gap * guess)
                    value = zed[:, lanes] * guess
                    total += value * value
                    value = jnp.where(source[o, :] == count[:, lanes], 1.0, value * keep[o, :])
                    c_high[t, into, lanes], c_low[t, into, lanes] = split(value)
                squares[o, :] = total
        for t in range(width // TILE):
            o = slice(t * TILE, (t + 1) * TILE)
            acc[half, o, :] += dot3((c_high[t], c_low[t]), (q_high[...], q_low[...]), (1, 0))

    def run(steps, place):
        def one(i, carry):
            dy, dx, half = place(i)
            unit(slot(dy, dx), half)
            return carry

        lax.fori_loop(0, steps, one, 0)

    def arrive(name, dy, dx, half):
        started[name].wait_recv()
        relay(("twin", dy, dx, half), dy, dx, half, twin)

    def ready(*places):
        for dy, dx, half in places:
            started["twin", dy, dx, half].wait_recv()

    ready((0, 0, 0), (0, 0, 1))
    run(2, lambda i: (0, 0, i))

    w_copy.wait()
    spot = wall.at[c, x, y]
    wall[c, x, y] = part[0, pl.ds(low * piece, piece), :] + x_in[0]
    for d in range(1, 4):
        ship(("w", d), spot, spot, dev(d, 0, 0))

    arrive(("up", 0), 3, 0, 0)
    relay(("up2", 0), 3, 0, 0, up)
    arrive(("down", 1), 1, 0, 1)
    relay(("down2", 1), 1, 0, 1, down)
    arrive(("over", 0), 0, 1, 0)
    relay(("upx", 0), 0, 1, 0, up)
    relay(("downx", 0), 0, 1, 0, down)
    ready((3, 0, 0), (1, 0, 1), (0, 1, 0))
    run(3, lambda i: (3 - 2 * i + i // 2, i // 2, lax.rem(i, 2)))

    for copy in cross_copies:
        copy.wait()
    mine = pl.ds(r * small, small)
    total = cross[mine, :]
    for d in range(1, 8):
        total += cross_in[lax.rem(r + d, 8)]
    cross_all[mine, :] = total
    cross_copies = row_copies(8, lambda to: cross_all.at[mine], cross_all.at[mine])

    arrive(("up", 1), 3, 0, 1)
    arrive(("down", 0), 1, 0, 0)
    for d in range(1, 4):
        started["w", d].wait_recv()
    ship("wx", wall.at[c, x], wall.at[c, x], over)
    arrive(("over", 1), 0, 1, 1)
    relay(("upx", 1), 0, 1, 1, up)
    relay(("downx", 1), 0, 1, 1, down)
    ready((3, 0, 1), (1, 0, 0), (0, 1, 1))
    run(3, lambda i: (3 - 2 * i + i // 2, i // 2, 1 - lax.rem(i, 2)))

    started["wx"].wait_recv()
    ship("wtwin", wall.at[c], wall.at[c], twin)
    arrive(("up2", 0), 2, 0, 0)
    relay(("over2", 0), 2, 0, 0, over)
    arrive(("down2", 1), 2, 0, 1)
    started["wtwin"].wait_recv()
    proj[1] = jnp.zeros(proj.shape[1:], F32)
    lax.fori_loop(0, 2, coefficients, 0)
    z_copies = scatter_z(24, 1)
    ready((2, 0, 0), (2, 0, 1))
    run(2, lambda i: (2, 0, i))
    z_copy = scatter_x(28, 1, z_copies)
    relay(("over2", 1), 2, 0, 1, over)

    arrive(("upx", 0), 3, 1, 0)
    arrive(("downx", 0), 1, 1, 0)
    ready((3, 1, 0), (1, 1, 0))
    run(1, lambda i: (3, 1, 0))

    for copy in cross_copies:
        copy.wait()
    z_copy.wait()
    mine = pl.ds(r * piece, piece)
    total = part[1, pl.ds(low * piece, piece), :] + x_in[1]
    order = [lax.broadcasted_iota(jnp.int32, (size, size), i) for i in range(2)]
    upper = [split(jnp.where(order[0] <= order[1], tri_ref[i], 0.0)) for i in range(2)]
    second = dot3(split(total[:, size:]), upper[1], (1, 1))
    rest = total[:, :size] - dot3(split(second), split(cross_all[...]), (1, 1))
    coef[mine, :size] = dot3(split(rest), upper[0], (1, 1))
    coef[mine, size:] = second
    to_x = one_row(29, coef.at[mine], coef.at[mine], z * 2 + 1 - low)
    run(1, lambda i: (1, 1, 0))
    to_x.wait()
    mine = pl.ds(z * 2 * piece, 2 * piece)
    to_z = []
    for d in range(1, 4):
        to = lax.rem(z + d, 4)
        to_z.append(one_row(29 + d, coef.at[mine], coef.at[mine], to * 2 + low))
    arrive(("over2", 0), 2, 1, 0)
    ready((2, 1, 0))
    run(1, lambda i: (2, 1, 0))

    arrive(("upx", 1), 3, 1, 1)
    arrive(("downx", 1), 1, 1, 1)
    arrive(("over2", 1), 2, 1, 1)
    ready((3, 1, 1), (1, 1, 1), (2, 1, 1))
    run(3, lambda i: (3 - 2 * i + 3 * (i // 2), 1, 1))

    for copy in to_z:
        copy.wait()
    norm = lax.rsqrt(jnp.sum(squares[...], axis=1, keepdims=True) + EPSILON)
    lam[...] = jnp.where(keep[...] > 0, norm, 1.0)
    out = []
    for half in range(2):
        sides = [split(vec_ref[block, half]) for block in range(2)]
        for t in range(width // TILE):
            o = slice(t * TILE, (t + 1) * TILE)
            value = acc[half, o, :]
            for block in range(2):
                some = split(coef[o, block * size : (block + 1) * size])
                value -= dot3(some, sides[block], (1, 1))
            acc[half, o, :] = value * lam[o, :1]
        copy = pltpu.make_async_copy(acc.at[half], turned_ref.at[half], local_sem.at[half])
        copy.start()
        out.append(copy)
    for copy in started.values():
        copy.wait_send()
    for copy in out:
        copy.wait()


def merge(q_turned, vectors, order, roots, poles, weights, deflated, triangles):
    depth, width = q_turned.shape[1], q_turned.shape[2]
    size = vectors.shape[3]
    vmem = pl.BlockSpec(memory_space=pltpu.VMEM)
    hbm = pl.BlockSpec(memory_space=pl.ANY)
    dma = pltpu.SemaphoreType.DMA
    span, piece = 2 * depth, width // 8
    scratch = [
        ((8, 2, 2, depth, width), F32),
        ((2, width, width), F32),
        ((16, span), F32),
        ((16, span), F32),
        ((2, span, 8), F32),
        ((2, span, 8), F32),
        ((8, width), F32),
        ((width, LANES), F32),
        ((width, LANES), F32),
        ((width, LANES), F32),
        ((width, LANES), F32),
        ((width // TILE, TILE, span), BF16),
        ((width // TILE, TILE, span), BF16),
        ((span, width), BF16),
        ((span, width), BF16),
        ((2, 2, 4, piece, 2 * size), F32),
        ((2, width, 2 * size), F32),
        ((2, 4, 2 * piece, 2 * size), F32),
        ((2, 2 * piece, 2 * size), F32),
        ((2, piece, 2 * size), F32),
        ((width, 2 * size), F32),
        ((size, size), F32),
        ((8, size // 8, size), F32),
        ((size, size), F32),
    ]
    return pl.pallas_call(
        merge_kernel,
        out_shape=jax.ShapeDtypeStruct((2, width, width), F32),
        in_specs=[hbm] + [vmem] * 7,
        out_specs=hbm,
        scratch_shapes=[pltpu.VMEM(*one) for one in scratch]
        + [dma((2,)), dma((40,)), dma((40,)), dma((40,)), dma((40,))],
        compiler_params=pltpu.CompilerParams(
            collective_id=0, has_side_effects=True, vmem_limit_bytes=60 * 1024 * 1024
        ),
        name="merge",
    )(q_turned, vectors, order, roots, poles, weights, deflated, triangles)


def turn_kernel(turned_ref, out_ref):
    out_ref[0] = turned_ref[0].T


def turn(turned):
    _, width, height = turned.shape
    return pl.pallas_call(
        turn_kernel,
        grid=(2, height // LANES),
        out_shape=jax.ShapeDtypeStruct((2, height, width), F32),
        in_specs=[pl.BlockSpec((1, width, LANES), lambda h, i: (h, 0, i))],
        out_specs=pl.BlockSpec((1, LANES, width), lambda h, i: (h, i, 0)),
        compiler_params=pltpu.CompilerParams(vmem_limit_bytes=60 * 1024 * 1024),
        name="turn",
    )(turned)


def local(
    q_halves, pole_values, weights, secular_roots, column_order, deflated, reflectors, triangles
):
    lines = (-1, LANES)
    turned = merge(
        jnp.swapaxes(q_halves, 1, 2),
        reflectors,
        column_order.reshape(lines),
        secular_roots.reshape(lines),
        pole_values.reshape(lines),
        weights.reshape(lines),
        deflated.reshape(lines),
        triangles,
    )
    return turn(turned)


def solution(mesh):
    placed = (P(None, "row", "col"), P(), P(), P(), P(), P(), P(None, None, "row", None), P())
    return jax.shard_map(
        local, mesh=mesh, in_specs=placed, out_specs=P(None, "row", "col"), check_vma=False
    )
```

```python
import functools

import jax
import jax.numpy as jnp
from jax import lax
from jax.experimental import pallas as pl
from jax.experimental.pallas import tpu as pltpu
from jax.sharding import PartitionSpec as P

EPSILON = 1e-06
MESH = pl.DeviceIdType.MESH
F32 = jnp.float32
BF16 = jnp.bfloat16
TILE = 320
LANES = 128
STRIP = 64


def split(value):
    high = value.astype(BF16)
    return high, (value - high.astype(F32)).astype(BF16)


def dot3(a, b, contract):
    dims = (((contract[0],), (contract[1],)), ((), ()))
    one = functools.partial(lax.dot_general, dimension_numbers=dims, preferred_element_type=F32)
    return one(a[0], b[0]) + one(a[0], b[1]) + one(a[1], b[0])


def merge_kernel(
    q_ref, vec_ref, order_ref, roots_ref, lines_ref, weights_ref, deflated_ref, tri_ref,
    turned_ref,
    panel, acc, poles_ref, zeds_ref, pole_cols, zed_cols, marks, source, lam, keep, squares,
    c_high, c_low, q_high, q_low, wall, proj, z_in, part, x_in, coef, cross, cross_in, cross_all,
    local_sem, send, recv, row_send, row_recv,
):
    r, col = lax.axis_index("row"), lax.axis_index("col")
    y, x, c = col // 4, lax.rem(col // 2, 2), lax.rem(col, 2)
    width = acc.shape[1]
    piece = width // 8
    z, low = r // 2, lax.rem(r, 2)
    size = vec_ref.shape[3]

    def dev(dy, dx, dc):
        return (r, lax.rem(y + dy, 4) * 4 + lax.rem(x + dx, 2) * 2 + lax.rem(c + dc, 2))

    def slot(dy, dx):
        return lax.rem(y + dy, 4) * 2 + lax.rem(x + dx, 2)

    up, down, over, twin = dev(1, 0, 0), dev(3, 0, 0), dev(0, 1, 0), dev(0, 0, 1)
    rows = [(lax.rem(r + d, 8), col) for d in range(1, 8)]

    barrier = pltpu.get_barrier_semaphore()
    for other in [up, down, dev(2, 0, 0), over, twin, *rows]:
        pl.semaphore_signal(barrier, inc=1, device_id=other, device_id_type=MESH)
    pl.semaphore_wait(barrier, 12)

    started = {}

    def ship(name, src, dst, to):
        at = len(started)
        copy = pltpu.make_async_remote_copy(
            src_ref=src, dst_ref=dst, send_sem=send.at[at], recv_sem=recv.at[at],
            device_id=to, device_id_type=MESH,
        )
        copy.start()
        started[name] = copy
        return copy

    def relay(name, dy, dx, half, to):
        place = panel.at[slot(dy, dx), half, c]
        ship(name, place, place, to)

    def ship_part(name, half, part_of, to):
        lines = pl.ds(part_of * (depth // 2), depth // 2)
        ship((name, part_of), q_ref.at[half, lines], panel.at[slot(0, 0), half, c, lines], to)

    def relay_part(name, dy, dx, half, part_of, to):
        lines = pl.ds(part_of * (depth // 2), depth // 2)
        place = panel.at[slot(dy, dx), half, c, lines]
        ship(name, place, place, to)

    own = []
    depth = panel.shape[3]
    for half in range(2):
        place = panel.at[slot(0, 0), half, c]
        mine = pltpu.make_async_copy(q_ref.at[half], place, local_sem.at[half])
        mine.start()
        own.append(mine)
    for name, half, to in (("up", 0, up), ("down", 1, down), ("over", 0, over)):
        ship((name, half), q_ref.at[half], panel.at[slot(0, 0), half, c], to)
    for half in range(2):
        ship(("twin", 0, 0, half), q_ref.at[half], panel.at[slot(0, 0), half, c], twin)
    for part_of in range(2):
        ship_part("up1", 1, part_of, up)
        ship_part("down0", 0, part_of, down)

    def row_copies(base, src_of, dst):
        copies = []
        for d in range(1, 8):
            to = lax.rem(r + d, 8)
            copy = pltpu.make_async_remote_copy(
                src_ref=src_of(to), dst_ref=dst, send_sem=row_send.at[base + d], recv_sem=row_recv.at[base + d],
                device_id=(to, col), device_id_type=MESH,
            )
            copy.start()
            copies.append(copy)
        return copies

    def one_row(at, src, dst, to):
        copy = pltpu.make_async_remote_copy(
            src_ref=src, dst_ref=dst, send_sem=row_send.at[at], recv_sem=row_recv.at[at],
            device_id=(to, col), device_id_type=MESH,
        )
        copy.start()
        return copy

    def scatter_z(base, which):
        copies = []
        for d in range(1, 4):
            to = lax.rem(z + d, 4)
            src = proj.at[which, pl.ds(to * 2 * piece, 2 * piece)]
            copies.append(one_row(base + d, src, z_in.at[which, z], to * 2 + low))
        return copies

    def scatter_x(base, which, copies):
        for copy in copies:
            copy.wait()
        total = proj[which, pl.ds(z * 2 * piece, 2 * piece), :]
        for d in range(1, 4):
            total += z_in[which, lax.rem(z + d, 4)]
        part[which] = total
        src = part.at[which, pl.ds((1 - low) * piece, piece)]
        return one_row(base, src, x_in.at[which], z * 2 + 1 - low)

    for half in range(2):
        own[half].wait()
        got = split(panel[slot(0, 0), half, c])
        for block in range(2):
            at = (0, slice(half * depth, (half + 1) * depth), slice(block * size, (block + 1) * size))
            proj[at] = dot3(got, split(vec_ref[block, half]), (1, 0))
    w_copies = scatter_z(16, 0)


    span = 2 * panel.shape[3]
    group = span // LANES
    for line in range(2 * panel.shape[0]):
        for i in range(group):
            at = slice(line * group + i, line * group + i + 1)
            into = (slice(line, line + 1), slice(i * LANES, (i + 1) * LANES))
            poles_ref[into] = lines_ref[at, :]
            zeds_ref[into] = weights_ref[at, :] * (1 - deflated_ref[at, :]).astype(F32)

    squares[...] = jnp.zeros(squares.shape, F32)
    acc[...] = jnp.zeros(acc.shape, F32)
    for i in range(width // LANES):
        own_line = order_ref[pl.ds(col * (width // LANES) + i, 1), :].astype(F32)
        source[i * LANES : (i + 1) * LANES, :] = jnp.broadcast_to(own_line, (LANES, LANES)).T

    def find(i, carry):
        o = pl.ds(pl.multiple_of(i * STRIP, STRIP), STRIP)
        wanted = source[o, :].astype(jnp.int32)

        def line(step, found):
            same = wanted == step * LANES + lax.broadcasted_iota(jnp.int32, (1, LANES), 1)
            flag = deflated_ref[pl.ds(step, 1), :].astype(F32)
            return (
                found[0] + jnp.where(same, roots_ref[pl.ds(step, 1), :], 0.0),
                found[1] + jnp.where(same, flag, 0.0),
            )

        zero = jnp.zeros((STRIP, LANES), F32)
        root, flag = lax.fori_loop(0, roots_ref.shape[0], line, (zero, zero))
        flag = jnp.sum(flag, axis=1, keepdims=True)
        lam[o, :] = jnp.broadcast_to(jnp.sum(root, axis=1, keepdims=True), (STRIP, LANES))
        keep[o, :] = jnp.broadcast_to(1.0 - flag, (STRIP, LANES))
        source[o, :] = jnp.where(flag > 0, source[o, :], -1.0)
        return carry

    lax.fori_loop(0, width // STRIP, find, 0)

    w_copy = scatter_x(20, 0, w_copies)
    for part_of in range(2):
        ship_part("over1", 1, part_of, over)
    for i in range(width // LANES):
        o = slice(i * LANES, (i + 1) * LANES)
        for line, values in enumerate((lam, keep, source)):
            marks[line : line + 1, o] = values[o, :].T[:1, :]
    for i in range(group):
        o = slice(i * LANES, (i + 1) * LANES)
        for half in range(2):
            pole_cols[half, o, :] = poles_ref[half * 8 : (half + 1) * 8, o].T
            zed_cols[half, o, :] = zeds_ref[half * 8 : (half + 1) * 8, o].T

    def coefficients(core, carry):
        half, first = r // 4, core * depth + lax.rem(r, 4) * piece
        lines = pl.ds(pl.multiple_of(first, 16), piece)
        inner = lax.broadcasted_iota(jnp.int32, (piece, 1), 0)
        for dx in range(2):
            for dy in range(4):
                m = dy * 2 + dx
                pole = pole_cols[half, lines, m : m + 1]
                zed = zed_cols[half, lines, m : m + 1]
                count = (half * 8 * span + m * span + first + inner).astype(F32)
                into = slice((dx * 4 + dy) * piece, (dx * 4 + dy + 1) * piece)
                for i in range(width // LANES):
                    o = slice(i * LANES, (i + 1) * LANES)
                    gap = pole - marks[0:1, o]
                    guess = pl.reciprocal(gap, approx=True)
                    guess = guess * (2.0 - gap * guess)
                    value = zed * guess * marks[1:2, o]
                    value = jnp.where(marks[2:3, o] == count, 1.0, value)
                    q_high[into, o], q_low[into, o] = split(value)
        w = split(wall[core].reshape(8 * piece, 2 * size))
        proj[1] += dot3((q_high[...], q_low[...]), w, (0, 0))
        return carry

    def unit(m, half):
        at = half * 8 + m
        pole = poles_ref[pl.ds(at, 1), :]
        zed = zeds_ref[pl.ds(at, 1), :]
        count = (at * span + lax.broadcasted_iota(jnp.int32, (1, span), 1)).astype(F32)
        q_high[...], q_low[...] = split(panel[m, half].reshape(span, width))
        for t in range(width // TILE):
            for i in range(TILE // STRIP):
                o = slice(t * TILE + i * STRIP, t * TILE + (i + 1) * STRIP)
                into = slice(i * STRIP, (i + 1) * STRIP)
                total = squares[o, :]
                for k in range(group):
                    lanes = slice(k * LANES, (k + 1) * LANES)
                    gap = pole[:, lanes] - lam[o, :]
                    guess = pl.reciprocal(gap, approx=True)
                    guess = guess * (2.0 - gap * guess)
                    value = zed[:, lanes] * guess
                    total += value * value
                    value = jnp.where(source[o, :] == count[:, lanes], 1.0, value * keep[o, :])
                    c_high[t, into, lanes], c_low[t, into, lanes] = split(value)
                squares[o, :] = total
        for t in range(width // TILE):
            o = slice(t * TILE, (t + 1) * TILE)
            acc[half, o, :] += dot3((c_high[t], c_low[t]), (q_high[...], q_low[...]), (1, 0))

    def run(steps, place):
        def one(i, carry):
            dy, dx, half = place(i)
            unit(slot(dy, dx), half)
            return carry

        lax.fori_loop(0, steps, one, 0)

    def arrive(name, dy, dx, half):
        started[name].wait_recv()
        relay(("twin", dy, dx, half), dy, dx, half, twin)

    def ready(*places):
        for dy, dx, half in places:
            started["twin", dy, dx, half].wait_recv()

    ready((0, 0, 0), (0, 0, 1))
    run(2, lambda i: (0, 0, i))

    w_copy.wait()
    spot = wall.at[c, x, y]
    wall[c, x, y] = part[0, pl.ds(low * piece, piece), :] + x_in[0]
    for d in range(1, 4):
        ship(("w", d), spot, spot, dev(d, 0, 0))

    arrive(("up", 0), 3, 0, 0)
    relay(("up2", 0), 3, 0, 0, up)
    arrive(("down", 1), 1, 0, 1)
    relay(("down2", 1), 1, 0, 1, down)
    arrive(("over", 0), 0, 1, 0)
    relay(("upx", 0), 0, 1, 0, up)
    relay(("downx", 0), 0, 1, 0, down)
    ready((3, 0, 0), (1, 0, 1), (0, 1, 0))
    run(3, lambda i: (3 - 2 * i + i // 2, i // 2, lax.rem(i, 2)))

    total = jnp.zeros(cross.shape, F32)
    for half in range(2):
        total += dot3(split(vec_ref[0, half]), split(vec_ref[1, half]), (0, 0))
    cross[...] = total

    small = cross.shape[0] // 8
    cross_copies = row_copies(0, lambda to: cross.at[pl.ds(to * small, small)], cross_in.at[r])

    started["up1", 0].wait_recv()
    arrive(("up1", 1), 3, 0, 1)
    started["down0", 0].wait_recv()
    arrive(("down0", 1), 1, 0, 0)
    ready((3, 0, 1), (1, 0, 0))
    run(2, lambda i: (3 - 2 * i, 0, 1 - i))
    for d in range(1, 4):
        started["w", d].wait_recv()
    ship("wx", wall.at[c, x], wall.at[c, x], over)

    started["over1", 0].wait_recv()
    arrive(("over1", 1), 0, 1, 1)
    relay(("upx", 1), 0, 1, 1, up)
    relay(("downx", 1), 0, 1, 1, down)
    ready((0, 1, 1))
    run(1, lambda i: (0, 1, 1))

    for copy in cross_copies:
        copy.wait()
    mine = pl.ds(r * small, small)
    total = cross[mine, :]
    for d in range(1, 8):
        total += cross_in[lax.rem(r + d, 8)]
    cross_all[mine, :] = total
    cross_copies = row_copies(8, lambda to: cross_all.at[mine], cross_all.at[mine])

    started["wx"].wait_recv()
    ship("wtwin", wall.at[c], wall.at[c], twin)
    arrive(("up2", 0), 2, 0, 0)
    relay(("over2", 0), 2, 0, 0, over)
    arrive(("down2", 1), 2, 0, 1)
    proj[1] = jnp.zeros(proj.shape[1:], F32)
    started["wtwin"].wait_recv()
    lax.fori_loop(0, 2, coefficients, 0)
    z_copies = scatter_z(24, 1)
    ready((2, 0, 0), (2, 0, 1))
    run(2, lambda i: (2, 0, i))
    z_copy = scatter_x(28, 1, z_copies)

    arrive(("upx", 0), 3, 1, 0)
    arrive(("downx", 0), 1, 1, 0)
    ready((3, 1, 0), (1, 1, 0))
    run(2, lambda i: (3 - 2 * i, 1, 0))

    for copy in cross_copies:
        copy.wait()
    z_copy.wait()
    mine = pl.ds(r * piece, piece)
    total = part[1, pl.ds(low * piece, piece), :] + x_in[1]
    order = [lax.broadcasted_iota(jnp.int32, (size, size), i) for i in range(2)]
    upper = [split(jnp.where(order[0] <= order[1], tri_ref[i], 0.0)) for i in range(2)]
    second = dot3(split(total[:, size:]), upper[1], (1, 1))
    rest = total[:, :size] - dot3(split(second), split(cross_all[...]), (1, 1))
    coef[mine, :size] = dot3(split(rest), upper[0], (1, 1))
    coef[mine, size:] = second
    to_x = one_row(29, coef.at[mine], coef.at[mine], z * 2 + 1 - low)
    arrive(("over2", 0), 2, 1, 0)
    to_x.wait()
    mine = pl.ds(z * 2 * piece, 2 * piece)
    to_z = []
    for d in range(1, 4):
        to = lax.rem(z + d, 4)
        to_z.append(one_row(29 + d, coef.at[mine], coef.at[mine], to * 2 + low))
    ready((2, 1, 0))
    run(1, lambda i: (2, 1, 0))

    arrive(("upx", 1), 3, 1, 1)
    relay_part("up3", 3, 1, 1, 0, up)
    arrive(("downx", 1), 1, 1, 1)
    relay_part("down3", 1, 1, 1, 1, down)
    ready((3, 1, 1), (1, 1, 1))
    run(2, lambda i: (3 - 2 * i, 1, 1))
    started["up3"].wait_recv()
    arrive("down3", 2, 1, 1)
    ready((2, 1, 1))
    run(1, lambda i: (2, 1, 1))

    for copy in to_z:
        copy.wait()
    norm = lax.rsqrt(jnp.sum(squares[...], axis=1, keepdims=True) + EPSILON)
    lam[...] = jnp.where(keep[...] > 0, norm, 1.0)
    out = []
    for half in range(2):
        sides = [split(vec_ref[block, half]) for block in range(2)]
        for t in range(width // TILE):
            o = slice(t * TILE, (t + 1) * TILE)
            value = acc[half, o, :]
            for block in range(2):
                some = split(coef[o, block * size : (block + 1) * size])
                value -= dot3(some, sides[block], (1, 1))
            acc[half, o, :] = value * lam[o, :1]
        copy = pltpu.make_async_copy(acc.at[half], turned_ref.at[half], local_sem.at[half])
        copy.start()
        out.append(copy)
    for copy in started.values():
        copy.wait_send()
    for copy in out:
        copy.wait()


def merge(q_turned, vectors, order, roots, poles, weights, deflated, triangles):
    depth, width = q_turned.shape[1], q_turned.shape[2]
    size = vectors.shape[3]
    vmem = pl.BlockSpec(memory_space=pltpu.VMEM)
    hbm = pl.BlockSpec(memory_space=pl.ANY)
    dma = pltpu.SemaphoreType.DMA
    span, piece = 2 * depth, width // 8
    scratch = [
        ((8, 2, 2, depth, width), F32),
        ((2, width, width), F32),
        ((16, span), F32),
        ((16, span), F32),
        ((2, span, 8), F32),
        ((2, span, 8), F32),
        ((8, width), F32),
        ((width, LANES), F32),
        ((width, LANES), F32),
        ((width, LANES), F32),
        ((width, LANES), F32),
        ((width // TILE, TILE, span), BF16),
        ((width // TILE, TILE, span), BF16),
        ((span, width), BF16),
        ((span, width), BF16),
        ((2, 2, 4, piece, 2 * size), F32),
        ((2, width, 2 * size), F32),
        ((2, 4, 2 * piece, 2 * size), F32),
        ((2, 2 * piece, 2 * size), F32),
        ((2, piece, 2 * size), F32),
        ((width, 2 * size), F32),
        ((size, size), F32),
        ((8, size // 8, size), F32),
        ((size, size), F32),
    ]
    return pl.pallas_call(
        merge_kernel,
        out_shape=jax.ShapeDtypeStruct((2, width, width), F32),
        in_specs=[hbm] + [vmem] * 7,
        out_specs=hbm,
        scratch_shapes=[pltpu.VMEM(*one) for one in scratch]
        + [dma((2,)), dma((40,)), dma((40,)), dma((40,)), dma((40,))],
        compiler_params=pltpu.CompilerParams(
            collective_id=0, has_side_effects=True, vmem_limit_bytes=60 * 1024 * 1024
        ),
        name="merge",
    )(q_turned, vectors, order, roots, poles, weights, deflated, triangles)


def turn_kernel(turned_ref, out_ref):
    out_ref[0] = turned_ref[0].T


def turn(turned):
    _, width, height = turned.shape
    return pl.pallas_call(
        turn_kernel,
        grid=(2,),
        out_shape=jax.ShapeDtypeStruct((2, height, width), F32),
        in_specs=[pl.BlockSpec((1, width, height), lambda h: (h, 0, 0))],
        out_specs=pl.BlockSpec((1, height, width), lambda h: (h, 0, 0)),
        compiler_params=pltpu.CompilerParams(vmem_limit_bytes=60 * 1024 * 1024),
        name="turn",
    )(turned)


def local(
    q_halves, pole_values, weights, secular_roots, column_order, deflated, reflectors, triangles
):
    lines = (-1, LANES)
    turned = merge(
        jnp.swapaxes(q_halves, 1, 2),
        reflectors,
        column_order.reshape(lines),
        secular_roots.reshape(lines),
        pole_values.reshape(lines),
        weights.reshape(lines),
        deflated.reshape(lines),
        triangles,
    )
    return turn(turned)


def solution(mesh):
    placed = (P(None, "row", "col"), P(), P(), P(), P(), P(), P(None, None, "row", None), P())
    return jax.shard_map(
        local, mesh=mesh, in_specs=placed, out_specs=P(None, "row", "col"), check_vma=False
    )
```

```python
import functools

import jax
import jax.numpy as jnp
from jax import lax
from jax.experimental import pallas as pl
from jax.experimental.pallas import tpu as pltpu
from jax.sharding import PartitionSpec as P

EPSILON = 1e-06
MESH = pl.DeviceIdType.MESH
F32 = jnp.float32
BF16 = jnp.bfloat16
TILE = 320
LANES = 128
STRIP = 64


def split(value):
    high = value.astype(BF16)
    return high, (value - high.astype(F32)).astype(BF16)


def dot3(a, b, contract):
    dims = (((contract[0],), (contract[1],)), ((), ()))
    one = functools.partial(lax.dot_general, dimension_numbers=dims, preferred_element_type=F32)
    return one(a[0], b[0]) + one(a[0], b[1]) + one(a[1], b[0])


def merge_kernel(
    q_ref, vec_ref, order_ref, roots_ref, lines_ref, weights_ref, deflated_ref, tri_ref,
    turned_ref,
    panel, acc, poles_ref, zeds_ref, pole_cols, zed_cols, marks, source, lam, keep, squares,
    c_high, c_low, q_high, q_low, wall, proj, z_in, part, x_in, coef, cross, cross_in, cross_all,
    local_sem, send, recv, row_send, row_recv,
):
    r, col = lax.axis_index("row"), lax.axis_index("col")
    y, x, c = col // 4, lax.rem(col // 2, 2), lax.rem(col, 2)
    width = acc.shape[1]
    piece = width // 8
    z, low = r // 2, lax.rem(r, 2)
    size = vec_ref.shape[3]

    def dev(dy, dx, dc):
        return (r, lax.rem(y + dy, 4) * 4 + lax.rem(x + dx, 2) * 2 + lax.rem(c + dc, 2))

    def slot(dy, dx):
        return lax.rem(y + dy, 4) * 2 + lax.rem(x + dx, 2)

    up, down, over, twin = dev(1, 0, 0), dev(3, 0, 0), dev(0, 1, 0), dev(0, 0, 1)
    rows = [(lax.rem(r + d, 8), col) for d in range(1, 8)]

    barrier = pltpu.get_barrier_semaphore()
    for other in [up, down, dev(2, 0, 0), over, twin, *rows]:
        pl.semaphore_signal(barrier, inc=1, device_id=other, device_id_type=MESH)
    pl.semaphore_wait(barrier, 12)

    started = {}

    def ship(name, src, dst, to):
        at = len(started)
        copy = pltpu.make_async_remote_copy(
            src_ref=src, dst_ref=dst, send_sem=send.at[at], recv_sem=recv.at[at],
            device_id=to, device_id_type=MESH,
        )
        copy.start()
        started[name] = copy
        return copy

    def relay(name, dy, dx, half, to):
        place = panel.at[slot(dy, dx), half, c]
        ship(name, place, place, to)

    def ship_part(name, half, part_of, to):
        lines = pl.ds(part_of * (depth // 2), depth // 2)
        ship((name, part_of), q_ref.at[half, lines], panel.at[slot(0, 0), half, c, lines], to)

    def relay_part(name, dy, dx, half, part_of, to):
        lines = pl.ds(part_of * (depth // 2), depth // 2)
        place = panel.at[slot(dy, dx), half, c, lines]
        ship(name, place, place, to)

    own = []
    depth = panel.shape[3]
    for half in range(2):
        place = panel.at[slot(0, 0), half, c]
        mine = pltpu.make_async_copy(q_ref.at[half], place, local_sem.at[half])
        mine.start()
        own.append(mine)
    for name, half, to in (("up", 0, up), ("down", 1, down), ("over", 0, over)):
        ship((name, half), q_ref.at[half], panel.at[slot(0, 0), half, c], to)
    for half in range(2):
        ship(("twin", 0, 0, half), q_ref.at[half], panel.at[slot(0, 0), half, c], twin)
    for part_of in range(2):
        ship_part("up1", 1, part_of, up)
        ship_part("down0", 0, part_of, down)

    def row_copies(base, src_of, dst):
        copies = []
        for d in range(1, 8):
            to = lax.rem(r + d, 8)
            copy = pltpu.make_async_remote_copy(
                src_ref=src_of(to), dst_ref=dst, send_sem=row_send.at[base + d], recv_sem=row_recv.at[base + d],
                device_id=(to, col), device_id_type=MESH,
            )
            copy.start()
            copies.append(copy)
        return copies

    def one_row(at, src, dst, to):
        copy = pltpu.make_async_remote_copy(
            src_ref=src, dst_ref=dst, send_sem=row_send.at[at], recv_sem=row_recv.at[at],
            device_id=(to, col), device_id_type=MESH,
        )
        copy.start()
        return copy

    def scatter_z(base, which):
        copies = []
        for d in range(1, 4):
            to = lax.rem(z + d, 4)
            src = proj.at[which, pl.ds(to * 2 * piece, 2 * piece)]
            copies.append(one_row(base + d, src, z_in.at[which, z], to * 2 + low))
        return copies

    def scatter_x(base, which, copies):
        for copy in copies:
            copy.wait()
        total = proj[which, pl.ds(z * 2 * piece, 2 * piece), :]
        for d in range(1, 4):
            total += z_in[which, lax.rem(z + d, 4)]
        part[which] = total
        src = part.at[which, pl.ds((1 - low) * piece, piece)]
        return one_row(base, src, x_in.at[which], z * 2 + 1 - low)

    for half in range(2):
        own[half].wait()
        got = split(panel[slot(0, 0), half, c])
        for block in range(2):
            at = (0, slice(half * depth, (half + 1) * depth), slice(block * size, (block + 1) * size))
            proj[at] = dot3(got, split(vec_ref[block, half]), (1, 0))
    w_copies = scatter_z(16, 0)


    span = 2 * panel.shape[3]
    group = span // LANES
    for line in range(2 * panel.shape[0]):
        for i in range(group):
            at = slice(line * group + i, line * group + i + 1)
            into = (slice(line, line + 1), slice(i * LANES, (i + 1) * LANES))
            poles_ref[into] = lines_ref[at, :]
            zeds_ref[into] = weights_ref[at, :] * (1 - deflated_ref[at, :]).astype(F32)

    squares[...] = jnp.zeros(squares.shape, F32)
    acc[...] = jnp.zeros(acc.shape, F32)
    for i in range(width // LANES):
        own_line = order_ref[pl.ds(col * (width // LANES) + i, 1), :].astype(F32)
        source[i * LANES : (i + 1) * LANES, :] = jnp.broadcast_to(own_line, (LANES, LANES)).T

    def find(i, carry):
        o = pl.ds(pl.multiple_of(i * STRIP, STRIP), STRIP)
        wanted = source[o, :].astype(jnp.int32)

        def line(step, found):
            same = wanted == step * LANES + lax.broadcasted_iota(jnp.int32, (1, LANES), 1)
            flag = deflated_ref[pl.ds(step, 1), :].astype(F32)
            return (
                found[0] + jnp.where(same, roots_ref[pl.ds(step, 1), :], 0.0),
                found[1] + jnp.where(same, flag, 0.0),
            )

        zero = jnp.zeros((STRIP, LANES), F32)
        root, flag = lax.fori_loop(0, roots_ref.shape[0], line, (zero, zero))
        flag = jnp.sum(flag, axis=1, keepdims=True)
        lam[o, :] = jnp.broadcast_to(jnp.sum(root, axis=1, keepdims=True), (STRIP, LANES))
        keep[o, :] = jnp.broadcast_to(1.0 - flag, (STRIP, LANES))
        source[o, :] = jnp.where(flag > 0, source[o, :], -1.0)
        return carry

    lax.fori_loop(0, width // STRIP, find, 0)

    w_copy = scatter_x(20, 0, w_copies)
    for part_of in range(2):
        ship_part("over1", 1, part_of, over)
    for i in range(width // LANES):
        o = slice(i * LANES, (i + 1) * LANES)
        for line, values in enumerate((lam, keep, source)):
            marks[line : line + 1, o] = values[o, :].T[:1, :]
    for i in range(group):
        o = slice(i * LANES, (i + 1) * LANES)
        for half in range(2):
            pole_cols[half, o, :] = poles_ref[half * 8 : (half + 1) * 8, o].T
            zed_cols[half, o, :] = zeds_ref[half * 8 : (half + 1) * 8, o].T

    def coefficients(core, carry):
        half, first = r // 4, core * depth + lax.rem(r, 4) * piece
        lines = pl.ds(pl.multiple_of(first, 16), piece)
        inner = lax.broadcasted_iota(jnp.int32, (piece, 1), 0)
        for dx in range(2):
            for dy in range(4):
                m = dy * 2 + dx
                pole = pole_cols[half, lines, m : m + 1]
                zed = zed_cols[half, lines, m : m + 1]
                count = (half * 8 * span + m * span + first + inner).astype(F32)
                into = slice((dx * 4 + dy) * piece, (dx * 4 + dy + 1) * piece)
                for i in range(width // LANES):
                    o = slice(i * LANES, (i + 1) * LANES)
                    gap = pole - marks[0:1, o]
                    guess = pl.reciprocal(gap, approx=True)
                    guess = guess * (2.0 - gap * guess)
                    value = zed * guess * marks[1:2, o]
                    value = jnp.where(marks[2:3, o] == count, 1.0, value)
                    q_high[into, o], q_low[into, o] = split(value)
        w = split(wall[core].reshape(8 * piece, 2 * size))
        proj[1] += dot3((q_high[...], q_low[...]), w, (0, 0))
        return carry

    def unit(m, half):
        at = half * 8 + m
        pole = poles_ref[pl.ds(at, 1), :]
        zed = zeds_ref[pl.ds(at, 1), :]
        count = (at * span + lax.broadcasted_iota(jnp.int32, (1, span), 1)).astype(F32)
        q_high[...], q_low[...] = split(panel[m, half].reshape(span, width))
        for t in range(width // TILE):
            for i in range(TILE // STRIP):
                o = slice(t * TILE + i * STRIP, t * TILE + (i + 1) * STRIP)
                into = slice(i * STRIP, (i + 1) * STRIP)
                total = squares[o, :]
                for k in range(group):
                    lanes = slice(k * LANES, (k + 1) * LANES)
                    gap = pole[:, lanes] - lam[o, :]
                    guess = pl.reciprocal(gap, approx=True)
                    guess = guess * (2.0 - gap * guess)
                    value = zed[:, lanes] * guess
                    total += value * value
                    value = jnp.where(source[o, :] == count[:, lanes], 1.0, value * keep[o, :])
                    c_high[t, into, lanes], c_low[t, into, lanes] = split(value)
                squares[o, :] = total
        for t in range(width // TILE):
            o = slice(t * TILE, (t + 1) * TILE)
            acc[half, o, :] += dot3((c_high[t], c_low[t]), (q_high[...], q_low[...]), (1, 0))

    def run(steps, place):
        def one(i, carry):
            dy, dx, half = place(i)
            unit(slot(dy, dx), half)
            return carry

        lax.fori_loop(0, steps, one, 0)

    def arrive(name, dy, dx, half):
        started[name].wait_recv()
        relay(("twin", dy, dx, half), dy, dx, half, twin)

    def ready(*places):
        for dy, dx, half in places:
            started["twin", dy, dx, half].wait_recv()

    ready((0, 0, 0), (0, 0, 1))
    run(2, lambda i: (0, 0, i))

    w_copy.wait()
    spot = wall.at[c, x, y]
    wall[c, x, y] = part[0, pl.ds(low * piece, piece), :] + x_in[0]
    for d in range(1, 4):
        ship(("w", d), spot, spot, dev(d, 0, 0))

    arrive(("up", 0), 3, 0, 0)
    relay(("up2", 0), 3, 0, 0, up)
    arrive(("down", 1), 1, 0, 1)
    relay(("down2", 1), 1, 0, 1, down)
    arrive(("over", 0), 0, 1, 0)
    relay(("upx", 0), 0, 1, 0, up)
    relay(("downx", 0), 0, 1, 0, down)
    ready((3, 0, 0), (1, 0, 1), (0, 1, 0))
    run(3, lambda i: (3 - 2 * i + i // 2, i // 2, lax.rem(i, 2)))

    total = jnp.zeros(cross.shape, F32)
    for half in range(2):
        total += dot3(split(vec_ref[0, half]), split(vec_ref[1, half]), (0, 0))
    cross[...] = total

    small = cross.shape[0] // 8
    cross_copies = row_copies(0, lambda to: cross.at[pl.ds(to * small, small)], cross_in.at[r])

    started["up1", 0].wait_recv()
    arrive(("up1", 1), 3, 0, 1)
    started["down0", 0].wait_recv()
    arrive(("down0", 1), 1, 0, 0)
    ready((3, 0, 1), (1, 0, 0))
    run(2, lambda i: (3 - 2 * i, 0, 1 - i))
    for d in range(1, 4):
        started["w", d].wait_recv()
    ship("wx", wall.at[c, x], wall.at[c, x], over)

    started["over1", 0].wait_recv()
    arrive(("over1", 1), 0, 1, 1)
    relay(("upx", 1), 0, 1, 1, up)
    relay(("downx", 1), 0, 1, 1, down)
    ready((0, 1, 1))
    run(1, lambda i: (0, 1, 1))

    for copy in cross_copies:
        copy.wait()
    mine = pl.ds(r * small, small)
    total = cross[mine, :]
    for d in range(1, 8):
        total += cross_in[lax.rem(r + d, 8)]
    cross_all[mine, :] = total
    cross_copies = row_copies(8, lambda to: cross_all.at[mine], cross_all.at[mine])

    started["wx"].wait_recv()
    ship("wtwin", wall.at[c], wall.at[c], twin)
    arrive(("up2", 0), 2, 0, 0)
    relay(("over2", 0), 2, 0, 0, over)
    arrive(("down2", 1), 2, 0, 1)
    proj[1] = jnp.zeros(proj.shape[1:], F32)
    started["wtwin"].wait_recv()
    lax.fori_loop(0, 2, coefficients, 0)
    z_copies = scatter_z(24, 1)
    ready((2, 0, 0), (2, 0, 1))
    run(2, lambda i: (2, 0, i))
    z_copy = scatter_x(28, 1, z_copies)

    arrive(("upx", 0), 3, 1, 0)
    arrive(("downx", 0), 1, 1, 0)
    ready((3, 1, 0), (1, 1, 0))
    run(2, lambda i: (3 - 2 * i, 1, 0))

    for copy in cross_copies:
        copy.wait()
    z_copy.wait()
    mine = pl.ds(r * piece, piece)
    total = part[1, pl.ds(low * piece, piece), :] + x_in[1]
    order = [lax.broadcasted_iota(jnp.int32, (size, size), i) for i in range(2)]
    upper = [split(jnp.where(order[0] <= order[1], tri_ref[i], 0.0)) for i in range(2)]
    second = dot3(split(total[:, size:]), upper[1], (1, 1))
    rest = total[:, :size] - dot3(split(second), split(cross_all[...]), (1, 1))
    coef[mine, :size] = dot3(split(rest), upper[0], (1, 1))
    coef[mine, size:] = second
    share_copies = row_copies(32, lambda to: coef.at[mine], coef.at[mine])
    arrive(("over2", 0), 2, 1, 0)
    ready((2, 1, 0))
    run(1, lambda i: (2, 1, 0))

    arrive(("upx", 1), 3, 1, 1)
    relay_part("up3", 3, 1, 1, 0, up)
    arrive(("downx", 1), 1, 1, 1)
    relay_part("down3", 1, 1, 1, 1, down)
    ready((3, 1, 1), (1, 1, 1))
    run(2, lambda i: (3 - 2 * i, 1, 1))
    started["up3"].wait_recv()
    arrive("down3", 2, 1, 1)
    ready((2, 1, 1))
    run(1, lambda i: (2, 1, 1))

    for copy in share_copies:
        copy.wait()
    norm = lax.rsqrt(jnp.sum(squares[...], axis=1, keepdims=True) + EPSILON)
    lam[...] = jnp.where(keep[...] > 0, norm, 1.0)
    out = []
    for half in range(2):
        sides = [split(vec_ref[block, half]) for block in range(2)]
        for t in range(width // TILE):
            o = slice(t * TILE, (t + 1) * TILE)
            value = acc[half, o, :]
            for block in range(2):
                some = split(coef[o, block * size : (block + 1) * size])
                value -= dot3(some, sides[block], (1, 1))
            acc[half, o, :] = value * lam[o, :1]
        copy = pltpu.make_async_copy(acc.at[half], turned_ref.at[half], local_sem.at[half])
        copy.start()
        out.append(copy)
    for copy in started.values():
        copy.wait_send()
    for copy in out:
        copy.wait()


def merge(q_turned, vectors, order, roots, poles, weights, deflated, triangles):
    depth, width = q_turned.shape[1], q_turned.shape[2]
    size = vectors.shape[3]
    vmem = pl.BlockSpec(memory_space=pltpu.VMEM)
    hbm = pl.BlockSpec(memory_space=pl.ANY)
    dma = pltpu.SemaphoreType.DMA
    span, piece = 2 * depth, width // 8
    scratch = [
        ((8, 2, 2, depth, width), F32),
        ((2, width, width), F32),
        ((16, span), F32),
        ((16, span), F32),
        ((2, span, 8), F32),
        ((2, span, 8), F32),
        ((8, width), F32),
        ((width, LANES), F32),
        ((width, LANES), F32),
        ((width, LANES), F32),
        ((width, LANES), F32),
        ((width // TILE, TILE, span), BF16),
        ((width // TILE, TILE, span), BF16),
        ((span, width), BF16),
        ((span, width), BF16),
        ((2, 2, 4, piece, 2 * size), F32),
        ((2, width, 2 * size), F32),
        ((2, 4, 2 * piece, 2 * size), F32),
        ((2, 2 * piece, 2 * size), F32),
        ((2, piece, 2 * size), F32),
        ((width, 2 * size), F32),
        ((size, size), F32),
        ((8, size // 8, size), F32),
        ((size, size), F32),
    ]
    return pl.pallas_call(
        merge_kernel,
        out_shape=jax.ShapeDtypeStruct((2, width, width), F32),
        in_specs=[hbm] + [vmem] * 7,
        out_specs=hbm,
        scratch_shapes=[pltpu.VMEM(*one) for one in scratch]
        + [dma((2,)), dma((40,)), dma((40,)), dma((40,)), dma((40,))],
        compiler_params=pltpu.CompilerParams(
            collective_id=0, has_side_effects=True, vmem_limit_bytes=60 * 1024 * 1024
        ),
        name="merge",
    )(q_turned, vectors, order, roots, poles, weights, deflated, triangles)


def turn_kernel(turned_ref, out_ref):
    out_ref[0] = turned_ref[0].T


def turn(turned):
    _, width, height = turned.shape
    return pl.pallas_call(
        turn_kernel,
        grid=(2,),
        out_shape=jax.ShapeDtypeStruct((2, height, width), F32),
        in_specs=[pl.BlockSpec((1, width, height), lambda h: (h, 0, 0))],
        out_specs=pl.BlockSpec((1, height, width), lambda h: (h, 0, 0)),
        compiler_params=pltpu.CompilerParams(vmem_limit_bytes=60 * 1024 * 1024),
        name="turn",
    )(turned)


def local(
    q_halves, pole_values, weights, secular_roots, column_order, deflated, reflectors, triangles
):
    lines = (-1, LANES)
    turned = merge(
        jnp.swapaxes(q_halves, 1, 2),
        reflectors,
        column_order.reshape(lines),
        secular_roots.reshape(lines),
        pole_values.reshape(lines),
        weights.reshape(lines),
        deflated.reshape(lines),
        triangles,
    )
    return turn(turned)


def solution(mesh):
    placed = (P(None, "row", "col"), P(), P(), P(), P(), P(), P(None, None, "row", None), P())
    return jax.shard_map(
        local, mesh=mesh, in_specs=placed, out_specs=P(None, "row", "col"), check_vma=False
    )
```

```python
import functools

import jax
import jax.numpy as jnp
from jax import lax
from jax.experimental import pallas as pl
from jax.experimental.pallas import tpu as pltpu
from jax.sharding import PartitionSpec as P

EPSILON = 1e-06
MESH = pl.DeviceIdType.MESH
F32 = jnp.float32
BF16 = jnp.bfloat16
TILE = 320
LANES = 128
STRIP = 64


def split(value):
    high = value.astype(BF16)
    return high, (value - high.astype(F32)).astype(BF16)


def dot3(a, b, contract):
    dims = (((contract[0],), (contract[1],)), ((), ()))
    one = functools.partial(lax.dot_general, dimension_numbers=dims, preferred_element_type=F32)
    return one(a[0], b[0]) + one(a[0], b[1]) + one(a[1], b[0])


def merge_kernel(
    q_ref, vec_ref, order_ref, roots_ref, lines_ref, weights_ref, deflated_ref, tri_ref,
    turned_ref,
    panel, acc, poles_ref, zeds_ref, pole_cols, zed_cols, marks, source, lam, keep, squares,
    c_high, c_low, q_high, q_low, wall, proj, z_in, part, x_in, coef, cross, cross_in, cross_all,
    local_sem, send, recv, row_send, row_recv,
):
    r, col = lax.axis_index("row"), lax.axis_index("col")
    y, x, c = col // 4, lax.rem(col // 2, 2), lax.rem(col, 2)
    width = acc.shape[1]
    piece = width // 8
    z, low = r // 2, lax.rem(r, 2)
    size = vec_ref.shape[3]

    def dev(dy, dx, dc):
        return (r, lax.rem(y + dy, 4) * 4 + lax.rem(x + dx, 2) * 2 + lax.rem(c + dc, 2))

    def slot(dy, dx):
        return lax.rem(y + dy, 4) * 2 + lax.rem(x + dx, 2)

    up, down, over, twin = dev(1, 0, 0), dev(3, 0, 0), dev(0, 1, 0), dev(0, 0, 1)
    rows = [(lax.rem(r + d, 8), col) for d in range(1, 8)]

    barrier = pltpu.get_barrier_semaphore()
    for other in [up, down, dev(2, 0, 0), over, twin, *rows]:
        pl.semaphore_signal(barrier, inc=1, device_id=other, device_id_type=MESH)
    pl.semaphore_wait(barrier, 12)

    started = {}

    def ship(name, src, dst, to):
        at = len(started)
        copy = pltpu.make_async_remote_copy(
            src_ref=src, dst_ref=dst, send_sem=send.at[at], recv_sem=recv.at[at],
            device_id=to, device_id_type=MESH,
        )
        copy.start()
        started[name] = copy
        return copy

    def relay(name, dy, dx, half, to):
        place = panel.at[slot(dy, dx), half, c]
        ship(name, place, place, to)

    def ship_part(name, half, part_of, to):
        lines = pl.ds(part_of * (depth // 2), depth // 2)
        ship((name, part_of), q_ref.at[half, lines], panel.at[slot(0, 0), half, c, lines], to)

    def relay_part(name, dy, dx, half, part_of, to):
        lines = pl.ds(part_of * (depth // 2), depth // 2)
        place = panel.at[slot(dy, dx), half, c, lines]
        ship(name, place, place, to)

    own = []
    depth = panel.shape[3]
    for half in range(2):
        place = panel.at[slot(0, 0), half, c]
        mine = pltpu.make_async_copy(q_ref.at[half], place, local_sem.at[half])
        mine.start()
        own.append(mine)
    for name, half, to in (("up", 0, up), ("down", 1, down), ("over", 0, over)):
        ship((name, half), q_ref.at[half], panel.at[slot(0, 0), half, c], to)
    for half in range(2):
        ship(("twin", 0, 0, half), q_ref.at[half], panel.at[slot(0, 0), half, c], twin)
    for part_of in range(2):
        ship_part("up1", 1, part_of, up)
        ship_part("down0", 0, part_of, down)

    def row_copies(base, src_of, dst):
        copies = []
        for d in range(1, 8):
            to = lax.rem(r + d, 8)
            copy = pltpu.make_async_remote_copy(
                src_ref=src_of(to), dst_ref=dst, send_sem=row_send.at[base + d], recv_sem=row_recv.at[base + d],
                device_id=(to, col), device_id_type=MESH,
            )
            copy.start()
            copies.append(copy)
        return copies

    def one_row(at, src, dst, to):
        copy = pltpu.make_async_remote_copy(
            src_ref=src, dst_ref=dst, send_sem=row_send.at[at], recv_sem=row_recv.at[at],
            device_id=(to, col), device_id_type=MESH,
        )
        copy.start()
        return copy

    def scatter_z(base, which):
        copies = []
        for d in range(1, 4):
            to = lax.rem(z + d, 4)
            src = proj.at[which, pl.ds(to * 2 * piece, 2 * piece)]
            copies.append(one_row(base + d, src, z_in.at[which, z], to * 2 + low))
        return copies

    def scatter_x(base, which, copies):
        for copy in copies:
            copy.wait()
        total = proj[which, pl.ds(z * 2 * piece, 2 * piece), :]
        for d in range(1, 4):
            total += z_in[which, lax.rem(z + d, 4)]
        part[which] = total
        src = part.at[which, pl.ds((1 - low) * piece, piece)]
        return one_row(base, src, x_in.at[which], z * 2 + 1 - low)

    for half in range(2):
        own[half].wait()
        got = split(panel[slot(0, 0), half, c])
        for block in range(2):
            at = (0, slice(half * depth, (half + 1) * depth), slice(block * size, (block + 1) * size))
            proj[at] = dot3(got, split(vec_ref[block, half]), (1, 0))
    w_copies = scatter_z(16, 0)


    span = 2 * panel.shape[3]
    group = span // LANES
    for line in range(2 * panel.shape[0]):
        for i in range(group):
            at = slice(line * group + i, line * group + i + 1)
            into = (slice(line, line + 1), slice(i * LANES, (i + 1) * LANES))
            poles_ref[into] = lines_ref[at, :]
            zeds_ref[into] = weights_ref[at, :] * (1 - deflated_ref[at, :]).astype(F32)

    squares[...] = jnp.zeros(squares.shape, F32)
    acc[...] = jnp.zeros(acc.shape, F32)
    for i in range(width // LANES):
        own_line = order_ref[pl.ds(col * (width // LANES) + i, 1), :].astype(F32)
        source[i * LANES : (i + 1) * LANES, :] = jnp.broadcast_to(own_line, (LANES, LANES)).T

    def find(i, carry):
        o = pl.ds(pl.multiple_of(i * STRIP, STRIP), STRIP)
        wanted = source[o, :].astype(jnp.int32)

        def line(step, found):
            same = wanted == step * LANES + lax.broadcasted_iota(jnp.int32, (1, LANES), 1)
            flag = deflated_ref[pl.ds(step, 1), :].astype(F32)
            return (
                found[0] + jnp.where(same, roots_ref[pl.ds(step, 1), :], 0.0),
                found[1] + jnp.where(same, flag, 0.0),
            )

        zero = jnp.zeros((STRIP, LANES), F32)
        root, flag = lax.fori_loop(0, roots_ref.shape[0], line, (zero, zero))
        flag = jnp.sum(flag, axis=1, keepdims=True)
        lam[o, :] = jnp.broadcast_to(jnp.sum(root, axis=1, keepdims=True), (STRIP, LANES))
        keep[o, :] = jnp.broadcast_to(1.0 - flag, (STRIP, LANES))
        source[o, :] = jnp.where(flag > 0, source[o, :], -1.0)
        return carry

    lax.fori_loop(0, width // STRIP, find, 0)

    w_copy = scatter_x(20, 0, w_copies)
    for part_of in range(2):
        ship_part("over1", 1, part_of, over)
    for i in range(width // LANES):
        o = slice(i * LANES, (i + 1) * LANES)
        for line, values in enumerate((lam, keep, source)):
            marks[line : line + 1, o] = values[o, :].T[:1, :]
    for i in range(group):
        o = slice(i * LANES, (i + 1) * LANES)
        for half in range(2):
            pole_cols[half, o, :] = poles_ref[half * 8 : (half + 1) * 8, o].T
            zed_cols[half, o, :] = zeds_ref[half * 8 : (half + 1) * 8, o].T

    def coefficients(core, carry):
        half, first = r // 4, core * depth + lax.rem(r, 4) * piece
        lines = pl.ds(pl.multiple_of(first, 16), piece)
        inner = lax.broadcasted_iota(jnp.int32, (piece, 1), 0)
        for dx in range(2):
            for dy in range(4):
                m = dy * 2 + dx
                pole = pole_cols[half, lines, m : m + 1]
                zed = zed_cols[half, lines, m : m + 1]
                count = (half * 8 * span + m * span + first + inner).astype(F32)
                into = slice((dx * 4 + dy) * piece, (dx * 4 + dy + 1) * piece)
                for i in range(width // LANES):
                    o = slice(i * LANES, (i + 1) * LANES)
                    gap = pole - marks[0:1, o]
                    guess = pl.reciprocal(gap, approx=True)
                    guess = guess * (2.0 - gap * guess)
                    value = zed * guess * marks[1:2, o]
                    value = jnp.where(marks[2:3, o] == count, 1.0, value)
                    q_high[into, o], q_low[into, o] = split(value)
        w = split(wall[core].reshape(8 * piece, 2 * size))
        proj[1] += dot3((q_high[...], q_low[...]), w, (0, 0))
        return carry

    def unit(m, half):
        at = half * 8 + m
        pole = poles_ref[pl.ds(at, 1), :]
        zed = zeds_ref[pl.ds(at, 1), :]
        count = (at * span + lax.broadcasted_iota(jnp.int32, (1, span), 1)).astype(F32)
        q_high[...], q_low[...] = split(panel[m, half].reshape(span, width))
        for t in range(width // TILE):
            for i in range(TILE // STRIP):
                o = slice(t * TILE + i * STRIP, t * TILE + (i + 1) * STRIP)
                into = slice(i * STRIP, (i + 1) * STRIP)
                total = squares[o, :]
                for k in range(group):
                    lanes = slice(k * LANES, (k + 1) * LANES)
                    gap = pole[:, lanes] - lam[o, :]
                    guess = pl.reciprocal(gap, approx=True)
                    guess = guess * (2.0 - gap * guess)
                    value = zed[:, lanes] * guess
                    total += value * value
                    value = jnp.where(source[o, :] == count[:, lanes], 1.0, value * keep[o, :])
                    c_high[t, into, lanes], c_low[t, into, lanes] = split(value)
                squares[o, :] = total
        for t in range(width // TILE):
            o = slice(t * TILE, (t + 1) * TILE)
            acc[half, o, :] += dot3((c_high[t], c_low[t]), (q_high[...], q_low[...]), (1, 0))

    def run(steps, place):
        def one(i, carry):
            dy, dx, half = place(i)
            unit(slot(dy, dx), half)
            return carry

        lax.fori_loop(0, steps, one, 0)

    def arrive(name, dy, dx, half):
        started[name].wait_recv()
        relay(("twin", dy, dx, half), dy, dx, half, twin)

    def ready(*places):
        for dy, dx, half in places:
            started["twin", dy, dx, half].wait_recv()

    ready((0, 0, 0), (0, 0, 1))
    run(2, lambda i: (0, 0, i))

    w_copy.wait()
    spot = wall.at[c, x, y]
    wall[c, x, y] = part[0, pl.ds(low * piece, piece), :] + x_in[0]
    for d in range(1, 4):
        ship(("w", d), spot, spot, dev(d, 0, 0))

    arrive(("up", 0), 3, 0, 0)
    relay(("up2", 0), 3, 0, 0, up)
    arrive(("down", 1), 1, 0, 1)
    relay(("down2", 1), 1, 0, 1, down)
    arrive(("over", 0), 0, 1, 0)
    relay(("upx", 0), 0, 1, 0, up)
    relay(("downx", 0), 0, 1, 0, down)
    ready((3, 0, 0), (1, 0, 1), (0, 1, 0))
    run(3, lambda i: (3 - 2 * i + i // 2, i // 2, lax.rem(i, 2)))

    total = jnp.zeros(cross.shape, F32)
    for half in range(2):
        total += dot3(split(vec_ref[0, half]), split(vec_ref[1, half]), (0, 0))
    cross[...] = total

    small = cross.shape[0] // 8
    cross_copies = row_copies(0, lambda to: cross.at[pl.ds(to * small, small)], cross_in.at[r])

    started["up1", 0].wait_recv()
    arrive(("up1", 1), 3, 0, 1)
    started["down0", 0].wait_recv()
    arrive(("down0", 1), 1, 0, 0)
    ready((3, 0, 1), (1, 0, 0))
    run(2, lambda i: (3 - 2 * i, 0, 1 - i))
    for d in range(1, 4):
        started["w", d].wait_recv()
    ship("wx", wall.at[c, x], wall.at[c, x], over)

    started["over1", 0].wait_recv()
    arrive(("over1", 1), 0, 1, 1)
    relay(("upx", 1), 0, 1, 1, up)
    relay(("downx", 1), 0, 1, 1, down)
    ready((0, 1, 1))
    run(1, lambda i: (0, 1, 1))

    for copy in cross_copies:
        copy.wait()
    mine = pl.ds(r * small, small)
    total = cross[mine, :]
    for d in range(1, 8):
        total += cross_in[lax.rem(r + d, 8)]
    cross_all[mine, :] = total
    cross_copies = row_copies(8, lambda to: cross_all.at[mine], cross_all.at[mine])

    started["wx"].wait_recv()
    ship("wtwin", wall.at[c], wall.at[c], twin)
    arrive(("up2", 0), 2, 0, 0)
    relay(("over2", 0), 2, 0, 0, over)
    arrive(("down2", 1), 2, 0, 1)
    proj[1] = jnp.zeros(proj.shape[1:], F32)
    started["wtwin"].wait_recv()
    lax.fori_loop(0, 2, coefficients, 0)
    z_copies = row_copies(
        24, lambda to: proj.at[1, pl.ds(to * piece, piece)], z_in.at[1, z, pl.ds(low * piece, piece)]
    )
    ready((2, 0, 0), (2, 0, 1))
    run(2, lambda i: (2, 0, i))

    arrive(("upx", 0), 3, 1, 0)
    arrive(("downx", 0), 1, 1, 0)
    ready((3, 1, 0), (1, 1, 0))
    run(2, lambda i: (3 - 2 * i, 1, 0))

    for copy in cross_copies:
        copy.wait()
    for copy in z_copies:
        copy.wait()
    mine = pl.ds(r * piece, piece)
    total = proj[1, mine, :]
    for d in range(1, 8):
        other = lax.rem(r + d, 8)
        total += z_in[1, other // 2, pl.ds(lax.rem(other, 2) * piece, piece), :]
    order = [lax.broadcasted_iota(jnp.int32, (size, size), i) for i in range(2)]
    upper = [split(jnp.where(order[0] <= order[1], tri_ref[i], 0.0)) for i in range(2)]
    second = dot3(split(total[:, size:]), upper[1], (1, 1))
    rest = total[:, :size] - dot3(split(second), split(cross_all[...]), (1, 1))
    coef[mine, :size] = dot3(split(rest), upper[0], (1, 1))
    coef[mine, size:] = second
    share_copies = row_copies(32, lambda to: coef.at[mine], coef.at[mine])
    arrive(("over2", 0), 2, 1, 0)
    ready((2, 1, 0))
    run(1, lambda i: (2, 1, 0))

    arrive(("upx", 1), 3, 1, 1)
    relay_part("up3", 3, 1, 1, 0, up)
    arrive(("downx", 1), 1, 1, 1)
    relay_part("down3", 1, 1, 1, 1, down)
    ready((3, 1, 1), (1, 1, 1))
    run(2, lambda i: (3 - 2 * i, 1, 1))
    started["up3"].wait_recv()
    arrive("down3", 2, 1, 1)
    ready((2, 1, 1))
    run(1, lambda i: (2, 1, 1))

    for copy in share_copies:
        copy.wait()
    norm = lax.rsqrt(jnp.sum(squares[...], axis=1, keepdims=True) + EPSILON)
    lam[...] = jnp.where(keep[...] > 0, norm, 1.0)
    out = []
    for half in range(2):
        sides = [split(vec_ref[block, half]) for block in range(2)]
        for t in range(width // TILE):
            o = slice(t * TILE, (t + 1) * TILE)
            value = acc[half, o, :]
            for block in range(2):
                some = split(coef[o, block * size : (block + 1) * size])
                value -= dot3(some, sides[block], (1, 1))
            acc[half, o, :] = value * lam[o, :1]
        copy = pltpu.make_async_copy(acc.at[half], turned_ref.at[half], local_sem.at[half])
        copy.start()
        out.append(copy)
    for copy in started.values():
        copy.wait_send()
    for copy in out:
        copy.wait()


def merge(q_turned, vectors, order, roots, poles, weights, deflated, triangles):
    depth, width = q_turned.shape[1], q_turned.shape[2]
    size = vectors.shape[3]
    vmem = pl.BlockSpec(memory_space=pltpu.VMEM)
    hbm = pl.BlockSpec(memory_space=pl.ANY)
    dma = pltpu.SemaphoreType.DMA
    span, piece = 2 * depth, width // 8
    scratch = [
        ((8, 2, 2, depth, width), F32),
        ((2, width, width), F32),
        ((16, span), F32),
        ((16, span), F32),
        ((2, span, 8), F32),
        ((2, span, 8), F32),
        ((8, width), F32),
        ((width, LANES), F32),
        ((width, LANES), F32),
        ((width, LANES), F32),
        ((width, LANES), F32),
        ((width // TILE, TILE, span), BF16),
        ((width // TILE, TILE, span), BF16),
        ((span, width), BF16),
        ((span, width), BF16),
        ((2, 2, 4, piece, 2 * size), F32),
        ((2, width, 2 * size), F32),
        ((2, 4, 2 * piece, 2 * size), F32),
        ((2, 2 * piece, 2 * size), F32),
        ((2, piece, 2 * size), F32),
        ((width, 2 * size), F32),
        ((size, size), F32),
        ((8, size // 8, size), F32),
        ((size, size), F32),
    ]
    return pl.pallas_call(
        merge_kernel,
        out_shape=jax.ShapeDtypeStruct((2, width, width), F32),
        in_specs=[hbm] + [vmem] * 7,
        out_specs=hbm,
        scratch_shapes=[pltpu.VMEM(*one) for one in scratch]
        + [dma((2,)), dma((40,)), dma((40,)), dma((40,)), dma((40,))],
        compiler_params=pltpu.CompilerParams(
            collective_id=0, has_side_effects=True, vmem_limit_bytes=60 * 1024 * 1024
        ),
        name="merge",
    )(q_turned, vectors, order, roots, poles, weights, deflated, triangles)


def turn_kernel(turned_ref, out_ref):
    out_ref[0] = turned_ref[0].T


def turn(turned):
    _, width, height = turned.shape
    return pl.pallas_call(
        turn_kernel,
        grid=(2,),
        out_shape=jax.ShapeDtypeStruct((2, height, width), F32),
        in_specs=[pl.BlockSpec((1, width, height), lambda h: (h, 0, 0))],
        out_specs=pl.BlockSpec((1, height, width), lambda h: (h, 0, 0)),
        compiler_params=pltpu.CompilerParams(vmem_limit_bytes=60 * 1024 * 1024),
        name="turn",
    )(turned)


def local(
    q_halves, pole_values, weights, secular_roots, column_order, deflated, reflectors, triangles
):
    lines = (-1, LANES)
    turned = merge(
        jnp.swapaxes(q_halves, 1, 2),
        reflectors,
        column_order.reshape(lines),
        secular_roots.reshape(lines),
        pole_values.reshape(lines),
        weights.reshape(lines),
        deflated.reshape(lines),
        triangles,
    )
    return turn(turned)


def solution(mesh):
    placed = (P(None, "row", "col"), P(), P(), P(), P(), P(), P(None, None, "row", None), P())
    return jax.shard_map(
        local, mesh=mesh, in_specs=placed, out_specs=P(None, "row", "col"), check_vma=False
    )
```

```python
import functools

import jax
import jax.numpy as jnp
from jax import lax
from jax.experimental import pallas as pl
from jax.experimental.pallas import tpu as pltpu
from jax.sharding import PartitionSpec as P

EPSILON = 1e-06
MESH = pl.DeviceIdType.MESH
F32 = jnp.float32
BF16 = jnp.bfloat16
TILE = 320
LANES = 128
STRIP = 64


def split(value):
    high = value.astype(BF16)
    return high, (value - high.astype(F32)).astype(BF16)


def dot3(a, b, contract):
    dims = (((contract[0],), (contract[1],)), ((), ()))
    one = functools.partial(lax.dot_general, dimension_numbers=dims, preferred_element_type=F32)
    return one(a[0], b[0]) + one(a[0], b[1]) + one(a[1], b[0])


def merge_kernel(
    q_ref, vec_ref, order_ref, roots_ref, lines_ref, weights_ref, deflated_ref, tri_ref,
    turned_ref,
    panel, acc, poles_ref, zeds_ref, pole_cols, zed_cols, marks, source, lam, keep, squares,
    c_high, c_low, q_high, q_low, wall, proj, z_in, part, x_in, coef, cross, cross_in, cross_all,
    local_sem, send, recv, row_send, row_recv,
):
    r, col = lax.axis_index("row"), lax.axis_index("col")
    y, x, c = col // 4, lax.rem(col // 2, 2), lax.rem(col, 2)
    width = acc.shape[1]
    piece = width // 8
    z, low = r // 2, lax.rem(r, 2)
    size = vec_ref.shape[3]

    def dev(dy, dx, dc):
        return (r, lax.rem(y + dy, 4) * 4 + lax.rem(x + dx, 2) * 2 + lax.rem(c + dc, 2))

    def slot(dy, dx):
        return lax.rem(y + dy, 4) * 2 + lax.rem(x + dx, 2)

    up, down, over, twin = dev(1, 0, 0), dev(3, 0, 0), dev(0, 1, 0), dev(0, 0, 1)
    rows = [(lax.rem(r + d, 8), col) for d in range(1, 8)]

    barrier = pltpu.get_barrier_semaphore()
    for other in [up, down, dev(2, 0, 0), over, twin, *rows]:
        pl.semaphore_signal(barrier, inc=1, device_id=other, device_id_type=MESH)
    pl.semaphore_wait(barrier, 12)

    started = {}

    def ship(name, src, dst, to):
        at = len(started)
        copy = pltpu.make_async_remote_copy(
            src_ref=src, dst_ref=dst, send_sem=send.at[at], recv_sem=recv.at[at],
            device_id=to, device_id_type=MESH,
        )
        copy.start()
        started[name] = copy
        return copy

    def relay(name, dy, dx, half, to):
        place = panel.at[slot(dy, dx), half, c]
        ship(name, place, place, to)

    def ship_part(name, half, part_of, to):
        lines = pl.ds(part_of * (depth // 2), depth // 2)
        ship((name, part_of), q_ref.at[half, lines], panel.at[slot(0, 0), half, c, lines], to)

    def relay_part(name, dy, dx, half, part_of, to):
        lines = pl.ds(part_of * (depth // 2), depth // 2)
        place = panel.at[slot(dy, dx), half, c, lines]
        ship(name, place, place, to)

    own = []
    depth = panel.shape[3]
    for half in range(2):
        place = panel.at[slot(0, 0), half, c]
        mine = pltpu.make_async_copy(q_ref.at[half], place, local_sem.at[half])
        mine.start()
        own.append(mine)
    for name, half, to in (("up", 0, up), ("down", 1, down), ("over", 0, over)):
        ship((name, half), q_ref.at[half], panel.at[slot(0, 0), half, c], to)
    for half in range(2):
        ship(("twin", 0, 0, half), q_ref.at[half], panel.at[slot(0, 0), half, c], twin)
    for part_of in range(2):
        ship_part("up1", 1, part_of, up)
        ship_part("down0", 0, part_of, down)

    def row_copies(base, src_of, dst):
        copies = []
        for d in range(1, 8):
            to = lax.rem(r + d, 8)
            copy = pltpu.make_async_remote_copy(
                src_ref=src_of(to), dst_ref=dst, send_sem=row_send.at[base + d], recv_sem=row_recv.at[base + d],
                device_id=(to, col), device_id_type=MESH,
            )
            copy.start()
            copies.append(copy)
        return copies

    def one_row(at, src, dst, to):
        copy = pltpu.make_async_remote_copy(
            src_ref=src, dst_ref=dst, send_sem=row_send.at[at], recv_sem=row_recv.at[at],
            device_id=(to, col), device_id_type=MESH,
        )
        copy.start()
        return copy

    def scatter_z(base, which):
        copies = []
        for d in range(1, 4):
            to = lax.rem(z + d, 4)
            src = proj.at[which, pl.ds(to * 2 * piece, 2 * piece)]
            copies.append(one_row(base + d, src, z_in.at[which, z], to * 2 + low))
        return copies

    def scatter_x(base, which, copies):
        for copy in copies:
            copy.wait()
        total = proj[which, pl.ds(z * 2 * piece, 2 * piece), :]
        for d in range(1, 4):
            total += z_in[which, lax.rem(z + d, 4)]
        part[which] = total
        src = part.at[which, pl.ds((1 - low) * piece, piece)]
        return one_row(base, src, x_in.at[which], z * 2 + 1 - low)

    for half in range(2):
        own[half].wait()
        got = split(panel[slot(0, 0), half, c])
        for block in range(2):
            at = (0, slice(half * depth, (half + 1) * depth), slice(block * size, (block + 1) * size))
            proj[at] = dot3(got, split(vec_ref[block, half]), (1, 0))
    w_copies = scatter_z(16, 0)


    span = 2 * panel.shape[3]
    group = span // LANES
    for line in range(2 * panel.shape[0]):
        for i in range(group):
            at = slice(line * group + i, line * group + i + 1)
            into = (slice(line, line + 1), slice(i * LANES, (i + 1) * LANES))
            poles_ref[into] = lines_ref[at, :]
            zeds_ref[into] = weights_ref[at, :] * (1 - deflated_ref[at, :]).astype(F32)

    squares[...] = jnp.zeros(squares.shape, F32)
    acc[...] = jnp.zeros(acc.shape, F32)
    for i in range(width // LANES):
        own_line = order_ref[pl.ds(col * (width // LANES) + i, 1), :].astype(F32)
        source[i * LANES : (i + 1) * LANES, :] = jnp.broadcast_to(own_line, (LANES, LANES)).T

    def find(i, carry):
        o = pl.ds(pl.multiple_of(i * STRIP, STRIP), STRIP)
        wanted = source[o, :].astype(jnp.int32)

        def line(step, found):
            same = wanted == step * LANES + lax.broadcasted_iota(jnp.int32, (1, LANES), 1)
            flag = deflated_ref[pl.ds(step, 1), :].astype(F32)
            return (
                found[0] + jnp.where(same, roots_ref[pl.ds(step, 1), :], 0.0),
                found[1] + jnp.where(same, flag, 0.0),
            )

        zero = jnp.zeros((STRIP, LANES), F32)
        root, flag = lax.fori_loop(0, roots_ref.shape[0], line, (zero, zero))
        flag = jnp.sum(flag, axis=1, keepdims=True)
        lam[o, :] = jnp.broadcast_to(jnp.sum(root, axis=1, keepdims=True), (STRIP, LANES))
        keep[o, :] = jnp.broadcast_to(1.0 - flag, (STRIP, LANES))
        source[o, :] = jnp.where(flag > 0, source[o, :], -1.0)
        return carry

    lax.fori_loop(0, width // STRIP, find, 0)

    w_copy = scatter_x(20, 0, w_copies)
    for part_of in range(2):
        ship_part("over1", 1, part_of, over)
    for i in range(width // LANES):
        o = slice(i * LANES, (i + 1) * LANES)
        for line, values in enumerate((lam, keep, source)):
            marks[line : line + 1, o] = values[o, :].T[:1, :]
    for i in range(group):
        o = slice(i * LANES, (i + 1) * LANES)
        for half in range(2):
            pole_cols[half, o, :] = poles_ref[half * 8 : (half + 1) * 8, o].T
            zed_cols[half, o, :] = zeds_ref[half * 8 : (half + 1) * 8, o].T

    def coefficients(core, carry):
        half, first = r // 4, core * depth + lax.rem(r, 4) * piece
        lines = pl.ds(pl.multiple_of(first, 16), piece)
        inner = lax.broadcasted_iota(jnp.int32, (piece, 1), 0)
        for dx in range(2):
            for dy in range(4):
                m = dy * 2 + dx
                pole = pole_cols[half, lines, m : m + 1]
                zed = zed_cols[half, lines, m : m + 1]
                count = (half * 8 * span + m * span + first + inner).astype(F32)
                into = slice((dx * 4 + dy) * piece, (dx * 4 + dy + 1) * piece)
                for i in range(width // LANES):
                    o = slice(i * LANES, (i + 1) * LANES)
                    gap = pole - marks[0:1, o]
                    guess = pl.reciprocal(gap, approx=True)
                    guess = guess * (2.0 - gap * guess)
                    value = zed * guess * marks[1:2, o]
                    value = jnp.where(marks[2:3, o] == count, 1.0, value)
                    q_high[into, o], q_low[into, o] = split(value)
        w = split(wall[core].reshape(8 * piece, 2 * size))
        proj[1] += dot3((q_high[...], q_low[...]), w, (0, 0))
        return carry

    def unit(m, half):
        at = half * 8 + m
        pole = poles_ref[pl.ds(at, 1), :]
        zed = zeds_ref[pl.ds(at, 1), :]
        count = (at * span + lax.broadcasted_iota(jnp.int32, (1, span), 1)).astype(F32)
        q_high[...], q_low[...] = split(panel[m, half].reshape(span, width))
        for t in range(width // TILE):
            for i in range(TILE // STRIP):
                o = slice(t * TILE + i * STRIP, t * TILE + (i + 1) * STRIP)
                into = slice(i * STRIP, (i + 1) * STRIP)
                total = squares[o, :]
                for k in range(group):
                    lanes = slice(k * LANES, (k + 1) * LANES)
                    gap = pole[:, lanes] - lam[o, :]
                    guess = pl.reciprocal(gap, approx=True)
                    guess = guess * (2.0 - gap * guess)
                    value = zed[:, lanes] * guess
                    total += value * value
                    value = jnp.where(source[o, :] == count[:, lanes], 1.0, value * keep[o, :])
                    c_high[t, into, lanes], c_low[t, into, lanes] = split(value)
                squares[o, :] = total
        for t in range(width // TILE):
            o = slice(t * TILE, (t + 1) * TILE)
            acc[half, o, :] += dot3((c_high[t], c_low[t]), (q_high[...], q_low[...]), (1, 0))

    def run(steps, place):
        def one(i, carry):
            dy, dx, half = place(i)
            unit(slot(dy, dx), half)
            return carry

        lax.fori_loop(0, steps, one, 0)

    def arrive(name, dy, dx, half):
        started[name].wait_recv()
        relay(("twin", dy, dx, half), dy, dx, half, twin)

    def ready(*places):
        for dy, dx, half in places:
            started["twin", dy, dx, half].wait_recv()

    ready((0, 0, 0), (0, 0, 1))
    run(2, lambda i: (0, 0, i))

    w_copy.wait()
    spot = wall.at[c, x, y]
    wall[c, x, y] = part[0, pl.ds(low * piece, piece), :] + x_in[0]
    for d in range(1, 4):
        ship(("w", d), spot, spot, dev(d, 0, 0))

    arrive(("up", 0), 3, 0, 0)
    relay(("up2", 0), 3, 0, 0, up)
    arrive(("down", 1), 1, 0, 1)
    relay(("down2", 1), 1, 0, 1, down)
    arrive(("over", 0), 0, 1, 0)
    relay(("upx", 0), 0, 1, 0, up)
    relay(("downx", 0), 0, 1, 0, down)
    ready((3, 0, 0), (1, 0, 1), (0, 1, 0))
    run(3, lambda i: (3 - 2 * i + i // 2, i // 2, lax.rem(i, 2)))

    total = jnp.zeros(cross.shape, F32)
    for half in range(2):
        total += dot3(split(vec_ref[0, half]), split(vec_ref[1, half]), (0, 0))
    cross[...] = total

    small = cross.shape[0] // 8
    cross_copies = row_copies(0, lambda to: cross.at[pl.ds(to * small, small)], cross_in.at[r])

    started["up1", 0].wait_recv()
    arrive(("up1", 1), 3, 0, 1)
    started["down0", 0].wait_recv()
    arrive(("down0", 1), 1, 0, 0)
    ready((3, 0, 1), (1, 0, 0))
    run(2, lambda i: (3 - 2 * i, 0, 1 - i))
    for d in range(1, 4):
        started["w", d].wait_recv()
    ship("wx", wall.at[c, x], wall.at[c, x], over)

    started["over1", 0].wait_recv()
    arrive(("over1", 1), 0, 1, 1)
    relay(("upx", 1), 0, 1, 1, up)
    relay(("downx", 1), 0, 1, 1, down)
    ready((0, 1, 1))
    run(1, lambda i: (0, 1, 1))

    for copy in cross_copies:
        copy.wait()
    mine = pl.ds(r * small, small)
    total = cross[mine, :]
    for d in range(1, 8):
        total += cross_in[lax.rem(r + d, 8)]
    cross_all[mine, :] = total
    cross_copies = row_copies(8, lambda to: cross_all.at[mine], cross_all.at[mine])

    started["wx"].wait_recv()
    ship("wtwin", wall.at[c], wall.at[c], twin)
    proj[1] = jnp.zeros(proj.shape[1:], F32)
    started["wtwin"].wait_recv()
    lax.fori_loop(0, 2, coefficients, 0)
    z_copies = row_copies(
        24, lambda to: proj.at[1, pl.ds(to * piece, piece)], z_in.at[1, z, pl.ds(low * piece, piece)]
    )
    arrive(("up2", 0), 2, 0, 0)
    relay(("over2", 0), 2, 0, 0, over)
    arrive(("down2", 1), 2, 0, 1)
    ready((2, 0, 0), (2, 0, 1))
    run(2, lambda i: (2, 0, i))

    arrive(("upx", 0), 3, 1, 0)
    arrive(("downx", 0), 1, 1, 0)
    ready((3, 1, 0), (1, 1, 0))
    run(2, lambda i: (3 - 2 * i, 1, 0))

    for copy in cross_copies:
        copy.wait()
    for copy in z_copies:
        copy.wait()
    mine = pl.ds(r * piece, piece)
    total = proj[1, mine, :]
    for d in range(1, 8):
        other = lax.rem(r + d, 8)
        total += z_in[1, other // 2, pl.ds(lax.rem(other, 2) * piece, piece), :]
    order = [lax.broadcasted_iota(jnp.int32, (size, size), i) for i in range(2)]
    upper = [split(jnp.where(order[0] <= order[1], tri_ref[i], 0.0)) for i in range(2)]
    second = dot3(split(total[:, size:]), upper[1], (1, 1))
    rest = total[:, :size] - dot3(split(second), split(cross_all[...]), (1, 1))
    coef[mine, :size] = dot3(split(rest), upper[0], (1, 1))
    coef[mine, size:] = second
    share_copies = row_copies(32, lambda to: coef.at[mine], coef.at[mine])
    arrive(("over2", 0), 2, 1, 0)
    ready((2, 1, 0))
    run(1, lambda i: (2, 1, 0))

    arrive(("upx", 1), 3, 1, 1)
    relay_part("up3", 3, 1, 1, 0, up)
    arrive(("downx", 1), 1, 1, 1)
    relay_part("down3", 1, 1, 1, 1, down)
    ready((3, 1, 1), (1, 1, 1))
    run(2, lambda i: (3 - 2 * i, 1, 1))
    started["up3"].wait_recv()
    arrive("down3", 2, 1, 1)
    ready((2, 1, 1))
    run(1, lambda i: (2, 1, 1))

    for copy in share_copies:
        copy.wait()
    norm = lax.rsqrt(jnp.sum(squares[...], axis=1, keepdims=True) + EPSILON)
    lam[...] = jnp.where(keep[...] > 0, norm, 1.0)
    out = []
    for half in range(2):
        sides = [split(vec_ref[block, half]) for block in range(2)]
        for t in range(width // TILE):
            o = slice(t * TILE, (t + 1) * TILE)
            value = acc[half, o, :]
            for block in range(2):
                some = split(coef[o, block * size : (block + 1) * size])
                value -= dot3(some, sides[block], (1, 1))
            acc[half, o, :] = value * lam[o, :1]
        copy = pltpu.make_async_copy(acc.at[half], turned_ref.at[half], local_sem.at[half])
        copy.start()
        out.append(copy)
    for copy in started.values():
        copy.wait_send()
    for copy in out:
        copy.wait()


def merge(q_turned, vectors, order, roots, poles, weights, deflated, triangles):
    depth, width = q_turned.shape[1], q_turned.shape[2]
    size = vectors.shape[3]
    vmem = pl.BlockSpec(memory_space=pltpu.VMEM)
    hbm = pl.BlockSpec(memory_space=pl.ANY)
    dma = pltpu.SemaphoreType.DMA
    span, piece = 2 * depth, width // 8
    scratch = [
        ((8, 2, 2, depth, width), F32),
        ((2, width, width), F32),
        ((16, span), F32),
        ((16, span), F32),
        ((2, span, 8), F32),
        ((2, span, 8), F32),
        ((8, width), F32),
        ((width, LANES), F32),
        ((width, LANES), F32),
        ((width, LANES), F32),
        ((width, LANES), F32),
        ((width // TILE, TILE, span), BF16),
        ((width // TILE, TILE, span), BF16),
        ((span, width), BF16),
        ((span, width), BF16),
        ((2, 2, 4, piece, 2 * size), F32),
        ((2, width, 2 * size), F32),
        ((2, 4, 2 * piece, 2 * size), F32),
        ((2, 2 * piece, 2 * size), F32),
        ((2, piece, 2 * size), F32),
        ((width, 2 * size), F32),
        ((size, size), F32),
        ((8, size // 8, size), F32),
        ((size, size), F32),
    ]
    return pl.pallas_call(
        merge_kernel,
        out_shape=jax.ShapeDtypeStruct((2, width, width), F32),
        in_specs=[hbm] + [vmem] * 7,
        out_specs=hbm,
        scratch_shapes=[pltpu.VMEM(*one) for one in scratch]
        + [dma((2,)), dma((40,)), dma((40,)), dma((40,)), dma((40,))],
        compiler_params=pltpu.CompilerParams(
            collective_id=0, has_side_effects=True, vmem_limit_bytes=60 * 1024 * 1024
        ),
        name="merge",
    )(q_turned, vectors, order, roots, poles, weights, deflated, triangles)


def turn_kernel(turned_ref, out_ref):
    out_ref[0] = turned_ref[0].T


def turn(turned):
    _, width, height = turned.shape
    return pl.pallas_call(
        turn_kernel,
        grid=(2,),
        out_shape=jax.ShapeDtypeStruct((2, height, width), F32),
        in_specs=[pl.BlockSpec((1, width, height), lambda h: (h, 0, 0))],
        out_specs=pl.BlockSpec((1, height, width), lambda h: (h, 0, 0)),
        compiler_params=pltpu.CompilerParams(vmem_limit_bytes=60 * 1024 * 1024),
        name="turn",
    )(turned)


def local(
    q_halves, pole_values, weights, secular_roots, column_order, deflated, reflectors, triangles
):
    lines = (-1, LANES)
    turned = merge(
        jnp.swapaxes(q_halves, 1, 2),
        reflectors,
        column_order.reshape(lines),
        secular_roots.reshape(lines),
        pole_values.reshape(lines),
        weights.reshape(lines),
        deflated.reshape(lines),
        triangles,
    )
    return turn(turned)


def solution(mesh):
    placed = (P(None, "row", "col"), P(), P(), P(), P(), P(), P(None, None, "row", None), P())
    return jax.shard_map(
        local, mesh=mesh, in_specs=placed, out_specs=P(None, "row", "col"), check_vma=False
    )
```
